128 devices in a mesh: row: 16 (over x, z), col: 8 (over y, core).
Axes of the slice: x: 4, y: 4, z: 4, core: 2. Of those that a mesh axis runs over, the one named last changes fastest.
Arguments:
- grm: float32 [8, 2048, 16, 1024], P(None, 'row', None, 'col'), may hold values from -1 to 2, as said below
- dosages: bfloat16 [64, 8, 2048], P(None, None, 'row'), may hold values from -5 to 5
- slab_weight: float32 [1], replicated, may hold values from 0.05 to 0.2
- genetic_var: float32 [1], replicated, may hold values from 0.4 to 1.2
- noise_var: float32 [1], replicated, may hold values from 0.3 to 1
Outputs:
- factored: float32 [8, 2048, 16, 1024], P(None, 'row', None, 'col')
The draws below stay inside these ranges and needn't reach their ends.
Inputs may be any that keep to these rules, and one draw needn't show every extreme that they name: `grm`: symmetric and positive definite.
All inputs are finite; a program needn't handle non-finite values.
Results may differ from the reference program's by a relative error of at most 0.0015.
Values may be sent and summed in bfloat16 or wider, within the bound.
A program may use at most 128 MiB of HBM per device.

```python
import math
import jax
import jax.numpy as jnp
from jax import lax

N = 16384
NB = 128
MS = 64
PANELS = 2
PANEL = 512
LBR = 8
LBC = 16
N_ROW = 16


def draw_grm(key, part):
    key = jax.random.fold_in(key, 11)
    first, second = jax.random.split(key)
    spread = 0.3
    lower_diag = 0.7
    upper_diag = 1.3
    noise = jax.random.uniform(first, (N, N), jnp.float32, -1.0, 1.0)
    offdiag = (noise + noise.T) * (spread / math.sqrt(N))
    diagonal = jax.random.uniform(second, (N,), jnp.float32, lower_diag, upper_diag)
    index = jnp.arange(N)
    full = jnp.where(index[:, None] == index[None, :], diagonal[None, :], offdiag)
    return full.reshape(LBR, N // LBR, LBC, N // LBC)


def block_scale(stream_key, shape, pieces, smallest, top_value):
    gain = 1.0
    for position, shards_of in pieces:
        steps = jax.random.uniform(jax.random.fold_in(jax.random.fold_in(stream_key, 6), position), (shards_of,), jnp.float32, smallest / len(pieces), top_value / len(pieces))
        gain = gain * jnp.repeat(jnp.exp(steps), shape[position] // shards_of).reshape((-1,) + (1,) * (len(shape) - 1 - position))
    return gain


def normal_values(rng, shape, scale, bound, cuts=(), kind=jnp.bfloat16):
    array = jax.random.normal(rng, shape, jnp.float32) * scale
    if len(cuts) > 0:
        array = block_scale(rng, shape, cuts, -0.22, 0.18) * array
    return jnp.clip(array, min=-bound, max=bound).astype(kind)


def setup_inputs(seed: int = 0) -> dict:
    keys = jax.random.split(jax.random.key(seed), 6)
    return {
        "grm": draw_grm(jax.random.fold_in(keys[5], 71), 0),
        "dosages": normal_values(keys[1], (MS, LBR, N_ROW * NB), 1.0, 5.0, ((2, 16),)),
        "slab_weight": jnp.clip(jax.random.uniform(keys[2], (1,), jnp.float32, 0.05, 0.2), 0.05, 0.2),
        "genetic_var": jnp.clip(jax.random.uniform(keys[3], (1,), jnp.float32, 0.4, 1.2), 0.4, 1.2),
        "noise_var": jnp.clip(jax.random.uniform(keys[4], (1,), jnp.float32, 0.3, 1.0), 0.3, 1.0),
    }


def reference(grm, dosages, slab_weight, genetic_var, noise_var):
    g = grm.reshape(N, N)
    z = dosages.reshape(MS, N)
    product = jnp.dot(z.T.astype(jnp.float32), z.astype(jnp.float32), preferred_element_type=jnp.float32)
    index = jnp.arange(N)
    eye = (index[:, None] == index[None, :]).astype(jnp.float32)
    work = genetic_var[0] * (g + slab_weight[0] / MS * product) + noise_var[0] * eye
    for p in range(PANELS):
        s0 = p * PANEL
        s1 = s0 + PANEL
        factor = jnp.linalg.cholesky(work[s0:s1, s0:s1])
        left = lax.linalg.triangular_solve(factor, work[:, s0:s1], left_side=False, lower=True, transpose_a=True)
        tail = left[s1:]
        work = work.at[s1:, s1:].add(-jnp.dot(tail.astype(jnp.float32), tail.T.astype(jnp.float32), precision=lax.Precision.HIGHEST, preferred_element_type=jnp.float32))
        lowered = jnp.where(index[:, None] >= (s0 + jnp.arange(PANEL))[None, :], left, 0.0)
        work = work.at[:, s0:s1].set(lowered)
    return work.reshape(grm.shape)
```

```python
import functools

import jax
import jax.numpy as jnp
from jax import lax
from jax.experimental import pallas as pl
from jax.experimental.pallas import tpu as pltpu
from jax.sharding import PartitionSpec as P

NB = 128
MS = 64
PANEL = 512
BOTH = 1024
HI = lax.Precision.HIGHEST
F32 = jnp.float32
BF16 = jnp.bfloat16


def lane_bcast(x, j):
    return jnp.broadcast_to(x[:, j : j + 1], (8, 128))


def sub_bcast(x, i):
    return jnp.broadcast_to(x[i : i + 1, :], (8, 128))


def inverse_factor_128(slabs):
    lane = lax.broadcasted_iota(jnp.int32, (8, 128), 1)
    sub = lax.broadcasted_iota(jnp.int32, (8, 128), 0)
    slabs = list(slabs)
    for s in range(16):
        cols = {t: [lane_bcast(slabs[t], 8 * s + k) for k in range(8)] for t in range(s, 16)}
        b = {(i, k): sub_bcast(cols[s][k], i) for k in range(8) for i in range(k, 8)}
        here = (lane >= 8 * s) & (lane < 8 * s + 8)
        ident = (lane - 8 * s == sub).astype(F32)
        rp = jnp.where(here, ident, slabs[s])
        r = [sub_bcast(rp, i) for i in range(8)]
        inv = [None] * 8
        l = {}
        for j in range(8):
            inv[j] = 1.0 / b[j, j]
            for i in range(j + 1, 8):
                l[i, j] = b[i, j] * inv[j]
            for i in range(j + 1, 8):
                for m in range(j + 1, i + 1):
                    b[i, m] = b[i, m] - l[i, j] * b[m, j]
                r[i] = r[i] - l[i, j] * r[j]
        out = None
        for i in range(8):
            v = r[i] * lax.rsqrt(b[i, i])
            out = v if out is None else jnp.where(sub == i, v, out)
        w = [r[i] * inv[i] for i in range(8)]
        for j in range(7, 0, -1):
            for i in range(j):
                w[i] = w[i] - l[j, i] * w[j]
        slabs[s] = jnp.where(lane < 8 * s + 8, out, 0.0)
        for t in range(s + 1, 16):
            acc = cols[t][0] * w[0]
            for k in range(1, 8):
                acc = acc + cols[t][k] * w[k]
            slabs[t] = jnp.where(here, 0.0, slabs[t]) - acc
    return slabs


def factor_kernel(scal_ref, p_ref, zp_ref, v_ref):
    gv, sw, nv = scal_ref[0], scal_ref[1], scal_ref[2]
    n = BOTH
    nb = n // NB
    zp = zp_ref[...]
    for i in range(nb):
        s = lax.dot_general(zp[:, i * NB : (i + 1) * NB], zp, (((0,), (0,)), ((), ())), preferred_element_type=F32)
        row = lax.broadcasted_iota(jnp.int32, (NB, n), 0) + i * NB
        col = lax.broadcasted_iota(jnp.int32, (NB, n), 1)
        g = jnp.concatenate([p_ref[i, k] for k in range(nb)], axis=1)
        v_ref[i * NB : (i + 1) * NB, :] = gv * (g + sw / MS * s) + jnp.where(row == col, nv, 0.0)
    for k in range(nb):
        kb = k * NB
        slabs = [v_ref[kb + 8 * s : kb + 8 * s + 8, kb : kb + NB] for s in range(16)]
        vk = jnp.concatenate(inverse_factor_128(slabs), axis=0)
        parts = []
        if k > 0:
            parts.append(jnp.dot(vk, v_ref[kb : kb + NB, :kb], precision=HI, preferred_element_type=F32))
        parts.append(vk)
        if k < nb - 1:
            right = jnp.dot(vk, v_ref[kb : kb + NB, kb + NB :], precision=HI, preferred_element_type=F32)
            parts.append(right)
            u = jnp.concatenate(parts, axis=1)
            upd = lax.dot_general(right, u, (((0,), (0,)), ((), ())), precision=HI, preferred_element_type=F32)
            if k > 0:
                v_ref[kb + NB :, :kb] = v_ref[kb + NB :, :kb] - upd[:, :kb]
                v_ref[kb : kb + NB, :kb] = parts[0]
            v_ref[kb + NB :, kb : kb + NB] = -upd[:, kb : kb + NB]
            v_ref[kb + NB :, kb + NB :] = v_ref[kb + NB :, kb + NB :] - upd[:, kb + NB :]
            v_ref[kb : kb + NB, kb : kb + NB] = vk
            v_ref[kb : kb + NB, kb + NB :] = jnp.zeros((NB, n - kb - NB), F32)
        else:
            v_ref[kb : kb + NB, :] = jnp.concatenate(parts, axis=1)


def factor(scal, p_raw, zp):
    return pl.pallas_call(
        factor_kernel,
        out_shape=jax.ShapeDtypeStruct((BOTH, BOTH), F32),
        in_specs=[
            pl.BlockSpec(memory_space=pltpu.SMEM),
            pl.BlockSpec(memory_space=pltpu.VMEM),
            pl.BlockSpec(memory_space=pltpu.VMEM),
        ],
        out_specs=pl.BlockSpec(memory_space=pltpu.VMEM),
        compiler_params=pltpu.CompilerParams(vmem_limit_bytes=48 * 1024 * 1024),
        cost_estimate=pl.CostEstimate(flops=20_000_000_000, bytes_accessed=8_000_000, transcendentals=0),
        name="panel_factor",
    )(scal, p_raw, zp)


def split(x):
    hi = x.astype(BF16)
    return hi, (x - hi.astype(F32)).astype(BF16)


NN = (((1,), (0,)), ((), ()))
NT = (((1,), (1,)), ((), ()))
TN = (((0,), (0,)), ((), ()))


def dot3(ah, al, bh, bl, dims):
    d = functools.partial(lax.dot_general, dimension_numbers=dims, preferred_element_type=F32)
    return d(ah, bh) + (d(ah, bl) + d(al, bh))


def update_kernel(
    scal_ref, zr_ref, zp_ref, zc_ref, g_hbm, left_hbm, right_hbm, v_hbm, out_hbm,
    gbuf, abuf, rbuf, vbuf, vh, vl, ah, al, wh, wl, sems,
):
    gv, sw, nv = scal_ref[0], scal_ref[1], scal_ref[2]
    swn = sw / MS
    row = lax.axis_index("row")
    col = lax.axis_index("col")
    copies_v = pltpu.make_async_copy(v_hbm, vbuf, sems.at[0])
    copies_v.start()
    copies_l = [
        pltpu.make_async_copy(left_hbm.at[k], abuf.at[:, k * NB : (k + 1) * NB], sems.at[1 + k]) for k in range(8)
    ]
    for c in copies_l:
        c.start()
    copies_r = [
        pltpu.make_async_copy(
            right_hbm.at[8 * h + k], rbuf.at[:, h, :, k * NB : (k + 1) * NB], sems.at[9 + 8 * h + k]
        )
        for h in range(2)
        for k in range(8)
    ]
    copy_g = pltpu.make_async_copy(g_hbm, gbuf, sems.at[25])
    for c in copies_r:
        c.start()
    copy_g.start()

    zr = zr_ref[...]
    zp = zp_ref[...]
    copies_v.wait()
    for J in range(4):
        h, lo = split(vbuf[J * 256 : (J + 1) * 256, :])
        vh[J * 256 : (J + 1) * 256, :] = h
        vl[J * 256 : (J + 1) * 256, :] = lo
    for c in copies_l:
        c.wait()

    @pl.loop(0, 8)
    def _(rb):
        at = pl.ds(pl.multiple_of(rb * NB, NB), NB)
        s = lax.dot_general(zr_ref[:, at], zp, TN, preferred_element_type=F32)
        me = row + 16 * rb
        r_at = lax.broadcasted_iota(jnp.int32, (NB, BOTH), 0) + me * NB
        c_at = lax.broadcasted_iota(jnp.int32, (NB, BOTH), 1)
        a = gv * (abuf[at, :] + swn * s) + jnp.where(r_at == c_at, nv, 0.0)
        h, lo = split(a)
        ah[at, :] = h
        al[at, :] = lo

    for J in range(4):
        K = (J + 1) * 256
        js = slice(J * 256, (J + 1) * 256)
        abuf[:, js] = dot3(ah[:, :K], al[:, :K], vh[js, :K], vl[js, :K], NT)

    keep1 = jnp.where(row >= 4, 1.0, 0.0)
    keep2 = jnp.where(row >= 8, 1.0, 0.0)
    for rb in range(8):
        at = slice(rb * NB, (rb + 1) * NB)
        x = abuf[at, :]
        if rb == 0:
            c_at = lax.broadcasted_iota(jnp.int32, (NB, BOTH), 1)
            x = x * jnp.where(c_at < PANEL, keep1, keep2)
        h, lo = split(x)
        ah[at, :] = h
        al[at, :] = lo

    for J in range(4):
        js = slice(J * 256, (J + 1) * 256)
        K = slice(J * 256, BOTH)
        w = dot3(ah[:, K], al[:, K], vh[K, js], vl[K, js], NN)
        h, lo = split(w)
        wh[:, js] = h
        wl[:, js] = lo

    for c in copies_r:
        c.wait()
    copy_g.wait()
    g2 = gbuf.reshape(16384, NB)

    @pl.loop(0, 8)
    def _(p):
        zc = zc_ref[:, pl.ds(pl.multiple_of(p * 256, 256), 256)]
        s = lax.dot_general(zc, zp, TN, preferred_element_type=F32)
        raw = jnp.concatenate([rbuf[p, 0], rbuf[p, 1]], axis=0)
        rh, rl = split(gv * (raw + swn * s))
        upd = dot3(wh[...], wl[...], rh, rl, NT)
        own = lax.dot_general(zr, zc, TN, preferred_element_type=F32)
        eye = jnp.where(
            lax.broadcasted_iota(jnp.int32, (NB, NB), 0) == lax.broadcasted_iota(jnp.int32, (NB, NB), 1), nv, 0.0
        )
        for rb in range(8):
            rs = slice(rb * NB, (rb + 1) * NB)
            for e in range(2):
                es = slice(e * NB, (e + 1) * NB)
                lc = 2 * p + e
                at = pl.ds(rb * 2048 + lc, NB, stride=16)
                on = jnp.where(16 * rb + row == 8 * lc + col, 1.0, 0.0)
                g2[at, :] = gv * (g2[at, :] + swn * own[rs, es]) - upd[rs, es] + on * eye

    r_at = lax.broadcasted_iota(jnp.int32, (NB, NB), 0) + row * NB
    c_at = lax.broadcasted_iota(jnp.int32, (NB, NB), 1) + col * NB
    mine = pl.ds(pl.multiple_of(col * NB, NB), NB)
    for rb in range(8):
        x = abuf[rb * NB : (rb + 1) * NB, mine]
        if rb == 0:
            x = jnp.where(r_at >= c_at, x, 0.0)
        g2[pl.ds(rb * 2048, NB, stride=16), :] = x
    done = pltpu.make_async_copy(gbuf, out_hbm, sems.at[26])
    done.start()
    done.wait()


def update(scal, zr, zp, zc, g, left, right, v):
    anyspec = pl.BlockSpec(memory_space=pl.ANY)
    vmem = pl.BlockSpec(memory_space=pltpu.VMEM)
    return pl.pallas_call(
        update_kernel,
        out_shape=jax.ShapeDtypeStruct((1024, 16, NB), F32),
        in_specs=[pl.BlockSpec(memory_space=pltpu.SMEM), vmem, vmem, vmem, anyspec, anyspec, anyspec, anyspec],
        out_specs=anyspec,
        scratch_shapes=[
            pltpu.VMEM((1024, 16, NB), F32),
            pltpu.VMEM((1024, BOTH), F32),
            pltpu.VMEM((8, 2, NB, BOTH), F32),
            pltpu.VMEM((BOTH, BOTH), F32),
            pltpu.VMEM((BOTH, BOTH), BF16),
            pltpu.VMEM((BOTH, BOTH), BF16),
            pltpu.VMEM((1024, BOTH), BF16),
            pltpu.VMEM((1024, BOTH), BF16),
            pltpu.VMEM((1024, BOTH), BF16),
            pltpu.VMEM((1024, BOTH), BF16),
            pltpu.SemaphoreType.DMA((27,)),
        ],
        compiler_params=pltpu.CompilerParams(vmem_limit_bytes=60 * 1024 * 1024),
        cost_estimate=pl.CostEstimate(flops=25_000_000_000, bytes_accessed=36_000_000, transcendentals=0),
        name="trailing_update",
    )(scal, zr, zp, zc, g, left, right, v)


TRANSPOSE = [((8 * h + c) * 8 + k, (8 * h + k) * 8 + c) for h in range(2) for c in range(8) for k in range(8)]


def per_device(grm, dosages, slab_weight, genetic_var, noise_var):
    mycol = lax.axis_index("col")
    scal = jnp.concatenate([genetic_var, slab_weight, noise_var])
    everyone = lax.all_gather(dosages, "row", axis=2, tiled=True)
    zr = dosages.reshape(MS, 1024)
    zp = everyone[:, 0, :BOTH]
    zc = lax.dynamic_slice_in_dim(everyone.reshape(MS, 16, 1024), mycol * NB, NB, 2).reshape(MS, 2048)
    block = grm[:, :, 0, :].reshape(1024, NB)
    left = lax.all_gather(block, "col", axis=0)
    p_raw = lax.all_gather(left[:, :NB, :], "row", axis=0)[:8]
    swapped = lax.ppermute(block, ("row", "col"), TRANSPOSE)
    right = lax.all_gather(swapped, "row", axis=0).reshape(16, 8, NB, NB)
    v = factor(scal, p_raw, zp)
    out = update(scal, zr, zp, zc, grm.reshape(1024, 16, NB), left, right, v)
    return out.reshape(grm.shape)


def solution(mesh):
    in_specs = (P(None, "row", None, "col"), P(None, None, "row"), P(), P(), P())
    out_specs = P(None, "row", None, "col")
    return jax.shard_map(
        per_device, mesh=mesh, in_specs=in_specs, out_specs=out_specs, check_vma=False
    )
```

```python
import functools

import jax
import jax.numpy as jnp
from jax import lax
from jax.experimental import pallas as pl
from jax.experimental.pallas import tpu as pltpu
from jax.sharding import PartitionSpec as P

NB = 128
MS = 64
PANEL = 512
BOTH = 1024
HI = lax.Precision.HIGHEST
F32 = jnp.float32
BF16 = jnp.bfloat16


def lane_bcast(x, j):
    return jnp.broadcast_to(x[:, j : j + 1], (8, 128))


def sub_bcast(x, i):
    return jnp.broadcast_to(x[i : i + 1, :], (8, 128))


def inverse_factor_128(slabs):
    lane = lax.broadcasted_iota(jnp.int32, (8, 128), 1)
    sub = lax.broadcasted_iota(jnp.int32, (8, 128), 0)
    slabs = list(slabs)
    for s in range(16):
        cols = {t: [lane_bcast(slabs[t], 8 * s + k) for k in range(8)] for t in range(s, 16)}
        b = {(i, k): sub_bcast(cols[s][k], i) for k in range(8) for i in range(k, 8)}
        here = (lane >= 8 * s) & (lane < 8 * s + 8)
        ident = (lane - 8 * s == sub).astype(F32)
        rp = jnp.where(here, ident, slabs[s])
        r = [sub_bcast(rp, i) for i in range(8)]
        inv = [None] * 8
        l = {}
        for j in range(8):
            inv[j] = 1.0 / b[j, j]
            for i in range(j + 1, 8):
                l[i, j] = b[i, j] * inv[j]
            for i in range(j + 1, 8):
                for m in range(j + 1, i + 1):
                    b[i, m] = b[i, m] - l[i, j] * b[m, j]
                r[i] = r[i] - l[i, j] * r[j]
        out = None
        for i in range(8):
            v = r[i] * lax.rsqrt(b[i, i])
            out = v if out is None else jnp.where(sub == i, v, out)
        w = [r[i] * inv[i] for i in range(8)]
        for j in range(7, 0, -1):
            for i in range(j):
                w[i] = w[i] - l[j, i] * w[j]
        slabs[s] = jnp.where(lane < 8 * s + 8, out, 0.0)
        for t in range(s + 1, 16):
            acc = cols[t][0] * w[0]
            for k in range(1, 8):
                acc = acc + cols[t][k] * w[k]
            slabs[t] = jnp.where(here, 0.0, slabs[t]) - acc
    return slabs


NN = (((1,), (0,)), ((), ()))
NT = (((1,), (1,)), ((), ()))
TN = (((0,), (0,)), ((), ()))
MESH = pl.DeviceIdType.MESH
ITEMS = 9


def split(x):
    hi = x.astype(BF16)
    return hi, (x - hi.astype(F32)).astype(BF16)


def dot3(ah, al, bh, bl, dims):
    d = functools.partial(lax.dot_general, dimension_numbers=dims, preferred_element_type=F32)
    return d(ah, bh) + (d(ah, bl) + d(al, bh))


def panel_kernel(
    scal_ref, zr_ref, g_hbm,
    wh, wl, lout, zp_out, left_hbm, right_hbm, zc_hbm,
    v_ref, ps, tmp, blk, zpb, dbuf, vkb, abuf, ah, al, vh, vl,
    xz_send, xz_recv, zp_send, zp_recv, zc_send, zc_recv, c_send, c_recv, q_send, q_recv, loc,
):
    gv, sw, nv = scal_ref[0], scal_ref[1], scal_ref[2]
    swn = sw / MS
    r = lax.axis_index("row")
    c = lax.axis_index("col")
    x, z = r // 4, r % 4
    core = c % 2

    barrier = pltpu.get_barrier_semaphore()
    for o in range(1, 16):
        pl.semaphore_signal(barrier, inc=1, device_id=((r + o) % 16, c), device_id_type=MESH)
    for o in range(1, 8):
        pl.semaphore_signal(barrier, inc=1, device_id=(r, (c + o) % 8), device_id_type=MESH)

    first = pltpu.make_async_copy(g_hbm.at[0:128, 0:8], tmp.at[0:128], loc.at[0])
    rest = pltpu.make_async_copy(g_hbm.at[128:1024, 0:8], tmp.at[128:1024], loc.at[1])
    first.start()
    rest.start()
    slab_copy = pltpu.make_async_copy(g_hbm.at[0:128], right_hbm.at[r % 8], loc.at[2])

    @pl.when(r < 8)
    def _():
        slab_copy.start()

    tmp2 = tmp.reshape(8192, NB)
    first.wait()
    blk[0:NB, :] = tmp2[pl.ds(0, NB, stride=8), :]

    @pl.when(r < 8)
    def _():
        ps[r % 8, c] = blk[0:NB, :]
        zpb[r % 8] = zr_ref[:, 0:NB]

    pl.semaphore_wait(barrier, 22)

    def rdma(src, dst, ssem, rsem, to):
        return pltpu.make_async_remote_copy(
            src_ref=src, dst_ref=dst, send_sem=ssem, recv_sem=rsem, device_id=to, device_id_type=MESH
        )

    rs = r % 8
    xz, zps, zcs = [], [], []
    for n, o in enumerate((8, 4, 12, 2, 6, 10, 14, 1, 3, 5, 7, 9, 11, 13, 15)):
        to = ((r + o) % 16, c)
        xz.append(rdma(ps.at[rs, c], ps.at[rs, c], xz_send.at[n], xz_recv.at[rs], to))
        zps.append(rdma(zpb.at[rs], zpb.at[rs], zp_send.at[n], zp_recv.at[rs], to))
        zcs.append(rdma(zr_ref, zc_hbm.at[r // 8], zc_send.at[n], zc_recv.at[r // 8], to))

    @pl.when(r < 8)
    def _():
        for n in range(15):
            xz[n].start()
        for n in range(15):
            zps[n].start()

    rest.wait()
    for rb in range(1, 8):
        blk[rb * NB : (rb + 1) * NB, :] = tmp2[pl.ds(rb * 1024, NB, stride=8), :]
    left_own = pltpu.make_async_copy(blk, left_hbm.at[c], loc.at[3])
    left_own.start()

    cp, cm, co, sib = (c + 2) % 8, (c + 6) % 8, (c + 4) % 8, c + 1 - 2 * core
    fwd_src = jnp.where(core == 0, cm, cp)
    fwd_to = jnp.where(core == 0, cp, cm)

    def at(i, k):
        return ps.at[i, k] if i < 8 else left_hbm.at[k]

    def gather(i):
        me = lambda k: at(i, k)
        own = blk if i == 8 else me(c)
        return dict(
            plus=rdma(own, me(c), c_send.at[i, 0], c_recv.at[i, 0], (r, cp)),
            minus=rdma(own, me(c), c_send.at[i, 1], c_recv.at[i, 1], (r, cm)),
            fwd=rdma(me(fwd_src), me(fwd_src), c_send.at[i, 2], c_recv.at[i, 2], (r, fwd_to)),
            s0=rdma(own, me(c), c_send.at[i, 3], c_recv.at[i, 3], (r, sib)),
            s1=rdma(me(cm), me(cm), c_send.at[i, 4], c_recv.at[i, 4], (r, sib)),
            s2=rdma(me(cp), me(cp), c_send.at[i, 5], c_recv.at[i, 5], (r, sib)),
            s3=rdma(me(co), me(co), c_send.at[i, 6], c_recv.at[i, 6], (r, sib)),
        )

    items = [gather(i) for i in range(ITEMS)]

    def e0(i):
        if i < 8:
            @pl.when(r != i)
            def _():
                rdma(ps.at[i, c], ps.at[i, c], xz_send.at[0], xz_recv.at[i], (r, sib)).wait_recv()
        for name in ("plus", "minus", "s0"):
            items[i][name].start()

    def e1(i):
        items[i]["plus"].wait_recv()
        items[i]["minus"].wait_recv()
        for name in ("fwd", "s1", "s2"):
            items[i][name].start()

    def e2(i):
        items[i]["fwd"].wait_recv()
        items[i]["s3"].start()

    def e3(i):
        for name in ("s0", "s1", "s2", "s3"):
            items[i][name].wait_recv()

    fs = jnp.where((x == 0) | (x == 3), 0, 1)
    up, down = x * 4 + (z + 1) % 4, x * 4 + (z + 3) % 4
    far = (3 - x) * 4 + z
    partner = (x + 1 - 2 * (x % 2)) * 4 + z

    def part(which, dz, h):
        s = 4 * (fs if which == 0 else 1 - fs) + (z + dz) % 4
        return right_hbm.at[s, :, 8 * h : 8 * h + 8]

    def q(n, h, ref, to):
        return rdma(ref, ref, q_send.at[n, h], q_recv.at[n, h], (to, c))

    Q = []
    for h in range(2):
        f_src = jnp.where(core == 0, (z + 3) % 4, (z + 1) % 4)
        f_to = jnp.where(core == 0, up, down)
        Q.append(
            dict(
                far=q(0, h, part(0, 0, h), far),
                mate=q(1, h, part(0, 0, h), partner),
                fu=q(2, h, part(0, 0, h), up),
                fd=q(3, h, part(0, 0, h), down),
                su=q(4, h, part(1, 0, h), up),
                sd=q(5, h, part(1, 0, h), down),
                ff=q(6, h, right_hbm.at[4 * fs + f_src, :, 8 * h : 8 * h + 8], f_to),
                sf=q(7, h, right_hbm.at[4 * (1 - fs) + f_src, :, 8 * h : 8 * h + 8], f_to),
            )
        )

    def r0():
        @pl.when(x < 2)
        def _():
            slab_copy.wait()
            for h in range(2):
                Q[h]["far"].start()

    def r1(h):
        @pl.when(x >= 2)
        def _():
            Q[h]["far"].wait_recv()
        for name in ("mate", "fu", "fd"):
            Q[h][name].start()

    def r2(h):
        Q[h]["mate"].wait_recv()
        Q[h]["su"].start()
        Q[h]["sd"].start()

    def r3(h):
        Q[h]["fu"].wait_recv()
        Q[h]["fd"].wait_recv()
        Q[h]["ff"].start()

    def r4(h):
        Q[h]["su"].wait_recv()
        Q[h]["sd"].wait_recv()
        Q[h]["sf"].start()

    def r5(h):
        Q[h]["ff"].wait_recv()
        Q[h]["sf"].wait_recv()

    for i in range(8):
        e0(i)
    r0()
    zc_own = pltpu.make_async_copy(zr_ref, zc_hbm.at[r // 8], loc.at[4])

    @pl.when(r % 8 == c)
    def _():
        zc_own.start()
        for n in range(15):
            zcs[n].start()

    for i in range(8):
        @pl.when(r != i)
        def _():
            rdma(zpb.at[i], zpb.at[i], zp_send.at[0], zp_recv.at[i], (r, sib)).wait_recv()
    zp = jnp.concatenate([zpb[i] for i in range(8)], axis=1)
    for i in range(8):
        zp_out[:, i * NB : (i + 1) * NB] = zpb[i]

    service = [
        (lambda: r1(0), ),
        (lambda: r1(1), lambda: e0(8)),
        (lambda: r2(0), ),
        (lambda: r2(1), ),
        (lambda: r3(0), ),
        (lambda: r3(1), ),
        (lambda: r4(0), ),
        (lambda: r4(1), ),
    ]

    def prepare(k):
        kb = k * NB
        n = BOTH - kb
        s = lax.dot_general(zp[:, kb : kb + NB], zp[:, kb:], TN, preferred_element_type=F32)
        g = jnp.concatenate([ps[k, j] for j in range(k, 8)], axis=1)
        on = lax.broadcasted_iota(jnp.int32, (NB, n), 0) == lax.broadcasted_iota(jnp.int32, (NB, n), 1)
        a = gv * (g + swn * s) + jnp.where(on, nv, 0.0)
        if k > 0:
            a = a + v_ref[kb : kb + NB, kb:]
        v_ref[kb : kb + NB, kb:] = a
        dbuf[...] = a[:, :NB]

    e1(0)
    e1(1)
    e2(0)
    e3(0)
    prepare(0)

    @pl.loop(0, 8)
    def _(k):
        slabs = [dbuf[8 * s : 8 * s + 8, :] for s in range(16)]
        for s, v in enumerate(inverse_factor_128(slabs)):
            vkb[8 * s : 8 * s + 8, :] = v
        for kk in range(8):
            @pl.when(k == kk)
            def _():
                kb = kk * NB
                vk = vkb[...]
                parts = []
                if kk > 0:
                    parts.append(jnp.dot(vk, v_ref[kb : kb + NB, :kb], precision=HI, preferred_element_type=F32))
                parts.append(vk)
                if kk < 7:
                    right = jnp.dot(vk, v_ref[kb : kb + NB, kb + NB :], precision=HI, preferred_element_type=F32)
                    parts.append(right)
                    u = jnp.concatenate(parts, axis=1)
                    upd = lax.dot_general(right, u, TN, precision=HI, preferred_element_type=F32)
                    if kk > 0:
                        v_ref[kb + NB :, :kb] = v_ref[kb + NB :, :kb] - upd[:, :kb]
                        v_ref[kb : kb + NB, :kb] = parts[0]
                        v_ref[kb + NB :, kb + NB :] = v_ref[kb + NB :, kb + NB :] - upd[:, kb + NB :]
                    else:
                        v_ref[kb + NB :, kb + NB :] = -upd[:, kb + NB :]
                    v_ref[kb + NB :, kb : kb + NB] = -upd[:, kb : kb + NB]
                    v_ref[kb : kb + NB, kb : kb + NB] = vk
                    v_ref[kb : kb + NB, kb + NB :] = jnp.zeros((NB, BOTH - kb - NB), F32)
                else:
                    v_ref[kb : kb + NB, :] = jnp.concatenate(parts, axis=1)
                for f in service[kk]:
                    f()
                if kk + 2 < ITEMS:
                    e1(kk + 2)
                if kk + 1 < ITEMS:
                    e2(kk + 1)
                if kk + 1 < 8:
                    e3(kk + 1)
                    prepare(kk + 1)

    left_own.wait()
    e3(8)
    pulls = [
        pltpu.make_async_copy(left_hbm.at[k], abuf.at[:, k * NB : (k + 1) * NB], loc.at[5 + k]) for k in range(8)
    ]
    for p in pulls:
        p.start()
    for J in range(4):
        js = slice(J * 256, (J + 1) * 256)
        h, lo = split(v_ref[js, :])
        vh[js, :] = h
        vl[js, :] = lo
    for p in pulls:
        p.wait()

    @pl.loop(0, 8)
    def _(rb):
        rows = pl.ds(pl.multiple_of(rb * NB, NB), NB)
        s = lax.dot_general(zr_ref[:, rows], zp_out[...], TN, preferred_element_type=F32)
        r_at = lax.broadcasted_iota(jnp.int32, (NB, BOTH), 0) + (r + 16 * rb) * NB
        c_at = lax.broadcasted_iota(jnp.int32, (NB, BOTH), 1)
        a = gv * (abuf[rows, :] + swn * s) + jnp.where(r_at == c_at, nv, 0.0)
        h, lo = split(a)
        ah[rows, :] = h
        al[rows, :] = lo

    for J in range(4):
        K = (J + 1) * 256
        js = slice(J * 256, (J + 1) * 256)
        abuf[:, js] = dot3(ah[:, :K], al[:, :K], vh[js, :K], vl[js, :K], NT)

    keep1 = jnp.where(r >= 4, 1.0, 0.0)
    keep2 = jnp.where(r >= 8, 1.0, 0.0)
    for rb in range(8):
        rows = slice(rb * NB, (rb + 1) * NB)
        a = abuf[rows, :]
        if rb == 0:
            c_at = lax.broadcasted_iota(jnp.int32, (NB, BOTH), 1)
            a = a * jnp.where(c_at < PANEL, keep1, keep2)
        h, lo = split(a)
        ah[rows, :] = h
        al[rows, :] = lo
    lout[...] = abuf[:, pl.ds(pl.multiple_of(c * NB, NB), NB)]

    for J in range(4):
        js = slice(J * 256, (J + 1) * 256)
        K = slice(J * 256, BOTH)
        h, lo = split(dot3(ah[:, K], al[:, K], vh[K, js], vl[K, js], NN))
        wh[:, js] = h
        wl[:, js] = lo

    for h in range(2):
        r5(h)

    @pl.when(r < 8)
    def _():
        for n in range(15):
            xz[n].wait_send()
            zps[n].wait_send()

    @pl.when(r % 8 == c)
    def _():
        zc_own.wait()
        for n in range(15):
            zcs[n].wait_send()

    for hh in range(2):
        @pl.when(r != c + 8 * hh)
        def _():
            rdma(zr_ref, zc_hbm.at[hh], zc_send.at[0], zc_recv.at[hh], (r, sib)).wait_recv()
    for i in range(ITEMS):
        for name in items[i]:
            items[i][name].wait_send()
    for h in range(2):
        @pl.when(x < 2)
        def _():
            Q[h]["far"].wait_send()
        for name in ("mate", "fu", "fd", "su", "sd", "ff", "sf"):
            Q[h][name].wait_send()


def panels(scal, zr, g):
    hbm = pl.BlockSpec(memory_space=pl.ANY)
    vmem = pl.BlockSpec(memory_space=pltpu.VMEM)
    dma = pltpu.SemaphoreType.DMA
    return pl.pallas_call(
        panel_kernel,
        out_shape=[
            jax.ShapeDtypeStruct((1024, BOTH), BF16),
            jax.ShapeDtypeStruct((1024, BOTH), BF16),
            jax.ShapeDtypeStruct((1024, NB), F32),
            jax.ShapeDtypeStruct((MS, BOTH), BF16),
            jax.ShapeDtypeStruct((8, 1024, NB), F32),
            jax.ShapeDtypeStruct((8, NB, 16, NB), F32),
            jax.ShapeDtypeStruct((2, MS, 1024), BF16),
        ],
        in_specs=[pl.BlockSpec(memory_space=pltpu.SMEM), vmem, hbm],
        out_specs=[vmem, vmem, vmem, vmem, hbm, hbm, hbm],
        scratch_shapes=[
            pltpu.VMEM((BOTH, BOTH), F32),
            pltpu.VMEM((8, 8, NB, NB), F32),
            pltpu.VMEM((1024, 8, NB), F32),
            pltpu.VMEM((1024, NB), F32),
            pltpu.VMEM((8, MS, NB), BF16),
            pltpu.VMEM((NB, NB), F32),
            pltpu.VMEM((NB, NB), F32),
            pltpu.VMEM((1024, BOTH), F32),
            pltpu.VMEM((1024, BOTH), BF16),
            pltpu.VMEM((1024, BOTH), BF16),
            pltpu.VMEM((BOTH, BOTH), BF16),
            pltpu.VMEM((BOTH, BOTH), BF16),
            dma((15,)), dma((8,)), dma((15,)), dma((8,)), dma((15,)), dma((2,)),
            dma((ITEMS, 7)), dma((ITEMS, 7)), dma((8, 2)), dma((8, 2)), dma((13,)),
        ],
        compiler_params=pltpu.CompilerParams(
            vmem_limit_bytes=60 * 1024 * 1024, collective_id=0, has_side_effects=True
        ),
        cost_estimate=pl.CostEstimate(flops=30_000_000_000, bytes_accessed=30_000_000, transcendentals=0),
        name="panel_factor",
    )(scal, zr, g)


def update_kernel(
    scal_ref, zr_ref, zp_ref, zc_ref, lblk_ref, g_hbm, right_hbm, wh_hbm, wl_hbm, out_hbm,
    gbuf, rbuf, wh, wl, sems,
):
    gv, sw, nv = scal_ref[0], scal_ref[1], scal_ref[2]
    swn = sw / MS
    row = lax.axis_index("row")
    col = lax.axis_index("col")
    loads = [
        pltpu.make_async_copy(wh_hbm, wh, sems.at[0]),
        pltpu.make_async_copy(wl_hbm, wl, sems.at[1]),
        pltpu.make_async_copy(right_hbm, rbuf, sems.at[2]),
        pltpu.make_async_copy(g_hbm, gbuf, sems.at[3]),
    ]
    for d in loads:
        d.start()
    for d in loads:
        d.wait()
    zr = zr_ref[...]
    zp = zp_ref[...]
    g2 = gbuf.reshape(16384, NB)
    r2 = rbuf.reshape(16384, NB)

    @pl.loop(0, 8)
    def _(p):
        where = pl.ds(pl.multiple_of(p * NB, NB), NB)
        zc = jnp.concatenate([zc_ref[0, :, where], zc_ref[1, :, where]], axis=1)
        s = lax.dot_general(zp, zc, TN, preferred_element_type=F32)
        raw = jnp.concatenate([r2[pl.ds(2 * p + e, BOTH, stride=16), :] for e in range(2)], axis=1)
        rh, rl = split(gv * (raw + swn * s))
        upd = dot3(wh[...], wl[...], rh, rl, NN)
        own = lax.dot_general(zr, zc, TN, preferred_element_type=F32)
        eye = jnp.where(
            lax.broadcasted_iota(jnp.int32, (NB, NB), 0) == lax.broadcasted_iota(jnp.int32, (NB, NB), 1), nv, 0.0
        )
        for rb in range(8):
            rows = slice(rb * NB, (rb + 1) * NB)
            for e in range(2):
                es = slice(e * NB, (e + 1) * NB)
                lc = 2 * p + e
                at = pl.ds(rb * 2048 + lc, NB, stride=16)
                on = jnp.where(16 * rb + row == 8 * lc + col, 1.0, 0.0)
                g2[at, :] = gv * (g2[at, :] + swn * own[rows, es]) - upd[rows, es] + on * eye

    r_at = lax.broadcasted_iota(jnp.int32, (NB, NB), 0) + row * NB
    c_at = lax.broadcasted_iota(jnp.int32, (NB, NB), 1) + col * NB
    for rb in range(8):
        x = lblk_ref[rb * NB : (rb + 1) * NB, :]
        if rb == 0:
            x = jnp.where(r_at >= c_at, x, 0.0)
        g2[pl.ds(rb * 2048, NB, stride=16), :] = x
    done = pltpu.make_async_copy(gbuf, out_hbm, sems.at[4])
    done.start()
    done.wait()


def update(scal, zr, zp, zc, lblk, g, right, wh, wl):
    hbm = pl.BlockSpec(memory_space=pl.ANY)
    vmem = pl.BlockSpec(memory_space=pltpu.VMEM)
    return pl.pallas_call(
        update_kernel,
        out_shape=jax.ShapeDtypeStruct((1024, 16, NB), F32),
        in_specs=[pl.BlockSpec(memory_space=pltpu.SMEM), vmem, vmem, vmem, vmem, hbm, hbm, hbm, hbm],
        out_specs=hbm,
        scratch_shapes=[
            pltpu.VMEM((1024, 16, NB), F32),
            pltpu.VMEM((1024, 16, NB), F32),
            pltpu.VMEM((1024, BOTH), BF16),
            pltpu.VMEM((1024, BOTH), BF16),
            pltpu.SemaphoreType.DMA((5,)),
        ],
        compiler_params=pltpu.CompilerParams(vmem_limit_bytes=60 * 1024 * 1024),
        cost_estimate=pl.CostEstimate(flops=15_000_000_000, bytes_accessed=30_000_000, transcendentals=0),
        name="trailing_update",
    )(scal, zr, zp, zc, lblk, g, right, wh, wl)


def per_device(grm, dosages, slab_weight, genetic_var, noise_var):
    scal = jnp.concatenate([genetic_var, slab_weight, noise_var])
    zr = dosages.reshape(MS, 1024)
    g = grm.reshape(1024, 16, NB)
    wh, wl, lblk, zp, _, right, zc = panels(scal, zr, g)
    out = update(scal, zr, zp, zc, lblk, g, right.reshape(1024, 16, NB), wh, wl)
    return out.reshape(grm.shape)


def solution(mesh):
    in_specs = (P(None, "row", None, "col"), P(None, None, "row"), P(), P(), P())
    out_specs = P(None, "row", None, "col")
    return jax.shard_map(
        per_device, mesh=mesh, in_specs=in_specs, out_specs=out_specs, check_vma=False
    )
```

```python
import functools

import jax
import jax.numpy as jnp
from jax import lax
from jax.experimental import pallas as pl
from jax.experimental.pallas import tpu as pltpu
from jax.sharding import PartitionSpec as P

NB = 128
MS = 64
PANEL = 512
BOTH = 1024
F32 = jnp.float32
BF16 = jnp.bfloat16


def lane_bcast(x, j):
    return jnp.broadcast_to(x[:, j : j + 1], (8, 128))


def sub_bcast(x, i):
    return jnp.broadcast_to(x[i : i + 1, :], (8, 128))


def inverse_factor_128(slabs):
    lane = lax.broadcasted_iota(jnp.int32, (8, 128), 1)
    sub = lax.broadcasted_iota(jnp.int32, (8, 128), 0)
    slabs = list(slabs)
    for s in range(16):
        cols = {t: [lane_bcast(slabs[t], 8 * s + k) for k in range(8)] for t in range(s, 16)}
        b = {(i, k): sub_bcast(cols[s][k], i) for k in range(8) for i in range(k, 8)}
        here = (lane >= 8 * s) & (lane < 8 * s + 8)
        ident = (lane - 8 * s == sub).astype(F32)
        rp = jnp.where(here, ident, slabs[s])
        r = [sub_bcast(rp, i) for i in range(8)]
        inv = [None] * 8
        l = {}
        if s < 15:
            nx = jnp.where(here, 0.0, slabs[s + 1])
            cn = list(cols[s + 1])
        for j in range(0, 8, 2):
            a, e, f = b[j, j], b[j + 1, j], b[j + 1, j + 1]
            rd = 1.0 / (a * f - e * e)
            inv[j] = 1.0 / a
            l[j + 1, j] = e * inv[j]
            inv[j + 1] = a * rd
            m0, m1 = {}, {}
            for i in range(j + 2, 8):
                m0[i] = (b[i, j] * f - b[i, j + 1] * e) * rd
                m1[i] = (b[i, j + 1] * a - b[i, j] * e) * rd
                l[i, j] = b[i, j] * inv[j]
                l[i, j + 1] = m1[i]
            for i in range(j + 2, 8):
                for m in range(j + 2, i + 1):
                    b[i, m] = b[i, m] - (m0[i] * b[m, j] + m1[i] * b[m, j + 1])
            for i in range(j + 2, 8):
                r[i] = r[i] - (m0[i] * r[j] + m1[i] * r[j + 1])
            if s < 15:
                q0 = (cn[j] * f - cn[j + 1] * e) * rd
                q1 = (cn[j + 1] * a - cn[j] * e) * rd
                nx = nx - (q0 * r[j] + q1 * r[j + 1])
                for i in range(j + 2, 8):
                    cn[i] = cn[i] - (m0[i] * cn[j] + m1[i] * cn[j + 1])
            r[j + 1] = r[j + 1] - l[j + 1, j] * r[j]
            b[j + 1, j + 1] = f - l[j + 1, j] * e
        out = None
        for i in range(8):
            v = r[i] * lax.rsqrt(b[i, i])
            out = v if out is None else jnp.where(sub == i, v, out)
        w = [r[i] * inv[i] for i in range(8)]
        for j in range(7, 0, -1):
            for i in range(j):
                w[i] = w[i] - l[j, i] * w[j]
        slabs[s] = jnp.where(lane < 8 * s + 8, out, 0.0)
        if s < 15:
            slabs[s + 1] = nx
        for t in range(s + 2, 16):
            acc = cols[t][0] * w[0]
            for k in range(1, 8):
                acc = acc + cols[t][k] * w[k]
            slabs[t] = jnp.where(here, 0.0, slabs[t]) - acc
    return slabs


NN = (((1,), (0,)), ((), ()))
NT = (((1,), (1,)), ((), ()))
TN = (((0,), (0,)), ((), ()))
MESH = pl.DeviceIdType.MESH
ITEMS = 9


def split(x):
    hi = x.astype(BF16)
    return hi, (x - hi.astype(F32)).astype(BF16)


def dot3(ah, al, bh, bl, dims):
    d = functools.partial(lax.dot_general, dimension_numbers=dims, preferred_element_type=F32)
    return d(ah, bh) + (d(ah, bl) + d(al, bh))


def panel_kernel(
    gv_ref, sw_ref, nv_ref, zr_ref, g_hbm,
    out_hbm,
    v_ref, ps, gbuf, blk, zpb, zcb, dbuf, vkb, lbuf, rbuf, abuf, ah, al, vh, vl, wh, wl, rh, rl, ub,
    xz_send, xz_recv, zp_send, zp_recv, zc_send, zc_recv, c_send, c_recv, q_send, q_recv, loc,
):
    gv, sw, nv = gv_ref[0], sw_ref[0], nv_ref[0]
    swn = sw / MS
    r = lax.axis_index("row")
    c = lax.axis_index("col")
    x, z = r // 4, r % 4
    core = c % 2

    barrier = pltpu.get_barrier_semaphore()
    for o in range(1, 16):
        pl.semaphore_signal(barrier, inc=1, device_id=((r + o) % 16, c), device_id_type=MESH)
    for o in range(1, 8):
        pl.semaphore_signal(barrier, inc=1, device_id=(r, (c + o) % 8), device_id_type=MESH)

    first = pltpu.make_async_copy(g_hbm.at[0:128], gbuf.at[0:128], loc.at[0])
    rest = pltpu.make_async_copy(g_hbm.at[128:1024], gbuf.at[128:1024], loc.at[1])
    first.start()
    rest.start()
    slab_copy = pltpu.make_async_copy(g_hbm.at[0:128], rbuf.at[r % 8], loc.at[2])

    @pl.when(r < 8)
    def _():
        slab_copy.start()

    g2 = gbuf.reshape(16384, NB)
    first.wait()
    blk[0:NB, :] = g2[pl.ds(0, NB, stride=16), :]

    @pl.when(r < 8)
    def _():
        ps[r % 8, c] = blk[0:NB, :]
        zpb[r % 8] = zr_ref[:, 0:NB]

    pl.semaphore_wait(barrier, 22)

    def rdma(src, dst, ssem, rsem, to):
        return pltpu.make_async_remote_copy(
            src_ref=src, dst_ref=dst, send_sem=ssem, recv_sem=rsem, device_id=to, device_id_type=MESH
        )

    rs = r % 8
    xz, zps, zcs = [], [], []
    for n, o in enumerate((8, 4, 12, 2, 6, 10, 14, 1, 3, 5, 7, 9, 11, 13, 15)):
        to = ((r + o) % 16, c)
        xz.append(rdma(ps.at[rs, c], ps.at[rs, c], xz_send.at[n], xz_recv.at[rs], to))
        zps.append(rdma(zpb.at[rs], zpb.at[rs], zp_send.at[n], zp_recv.at[rs], to))
        zcs.append(rdma(zr_ref, zcb.at[r // 8], zc_send.at[n], zc_recv.at[r // 8], to))

    @pl.when(r == 0)
    def _():
        for n in range(15):
            xz[n].start()

    @pl.when(r < 8)
    def _():
        for n in range(15):
            zps[n].start()

    def own_rows():
        rest.wait()
        for rb in range(1, 8):
            blk[rb * NB : (rb + 1) * NB, :] = g2[pl.ds(rb * 2048, NB, stride=16), :]
        lbuf[c] = blk[...]

    cp, cm, co, sib = (c + 2) % 8, (c + 6) % 8, (c + 4) % 8, c + 1 - 2 * core
    fwd_src = jnp.where(core == 0, cm, cp)
    fwd_to = jnp.where(core == 0, cp, cm)

    def at(i, k):
        return ps.at[i, k] if i < 8 else lbuf.at[k]

    def gather(i):
        me = lambda k: at(i, k)
        own = blk if i == 8 else me(c)
        return dict(
            plus=rdma(own, me(c), c_send.at[i, 0], c_recv.at[i, 0], (r, cp)),
            minus=rdma(own, me(c), c_send.at[i, 1], c_recv.at[i, 1], (r, cm)),
            fwd=rdma(me(fwd_src), me(fwd_src), c_send.at[i, 2], c_recv.at[i, 2], (r, fwd_to)),
            s0=rdma(own, me(c), c_send.at[i, 3], c_recv.at[i, 3], (r, sib)),
            s1=rdma(me(cm), me(cm), c_send.at[i, 4], c_recv.at[i, 4], (r, sib)),
            s2=rdma(me(cp), me(cp), c_send.at[i, 5], c_recv.at[i, 5], (r, sib)),
            s3=rdma(me(co), me(co), c_send.at[i, 6], c_recv.at[i, 6], (r, sib)),
        )

    items = [gather(i) for i in range(ITEMS)]

    def e0(i):
        if i < 8:
            @pl.when(r != i)
            def _():
                rdma(ps.at[i, c], ps.at[i, c], xz_send.at[0], xz_recv.at[i], (r, sib)).wait_recv()
        for name in ("plus", "minus", "s0"):
            items[i][name].start()

    def e1(i):
        items[i]["plus"].wait_recv()
        items[i]["minus"].wait_recv()
        for name in ("fwd", "s1", "s2"):
            items[i][name].start()

    def e2(i):
        items[i]["fwd"].wait_recv()
        items[i]["s3"].start()

    def e3(i):
        for name in ("s0", "s1", "s2", "s3"):
            items[i][name].wait_recv()

    fs = jnp.where((x == 0) | (x == 3), 0, 1)
    up, down = x * 4 + (z + 1) % 4, x * 4 + (z + 3) % 4
    far = (3 - x) * 4 + z
    partner = (x + 1 - 2 * (x % 2)) * 4 + z

    def part(which, dz, h):
        s = 4 * (fs if which == 0 else 1 - fs) + (z + dz) % 4
        return rbuf.at[s, :, 8 * h : 8 * h + 8]

    def q(n, h, ref, to):
        return rdma(ref, ref, q_send.at[n, h], q_recv.at[n, h], (to, c))

    Q = []
    for h in range(2):
        f_src = jnp.where(core == 0, (z + 3) % 4, (z + 1) % 4)
        f_to = jnp.where(core == 0, up, down)
        Q.append(
            dict(
                far=q(0, h, part(0, 0, h), far),
                mate=q(1, h, part(0, 0, h), partner),
                fu=q(2, h, part(0, 0, h), up),
                fd=q(3, h, part(0, 0, h), down),
                su=q(4, h, part(1, 0, h), up),
                sd=q(5, h, part(1, 0, h), down),
                ff=q(6, h, rbuf.at[4 * fs + f_src, :, 8 * h : 8 * h + 8], f_to),
                sf=q(7, h, rbuf.at[4 * (1 - fs) + f_src, :, 8 * h : 8 * h + 8], f_to),
            )
        )

    def r0():
        @pl.when(x < 2)
        def _():
            slab_copy.wait()
            for h in range(2):
                Q[h]["far"].start()

    def r1(h):
        @pl.when(x >= 2)
        def _():
            Q[h]["far"].wait_recv()
        for name in ("mate", "fu", "fd"):
            Q[h][name].start()

    def r2(h):
        Q[h]["mate"].wait_recv()
        Q[h]["su"].start()
        Q[h]["sd"].start()

    def r3(h):
        Q[h]["fu"].wait_recv()
        Q[h]["fd"].wait_recv()
        Q[h]["ff"].start()

    def r4(h):
        Q[h]["su"].wait_recv()
        Q[h]["sd"].wait_recv()
        Q[h]["sf"].start()

    def r5(h):
        Q[h]["ff"].wait_recv()
        Q[h]["sf"].wait_recv()

    e0(0)

    @pl.when((r > 0) & (r < 8))
    def _():
        for n in range(15):
            xz[n].start()

    zc_own = pltpu.make_async_copy(zr_ref, zcb.at[r // 8], loc.at[4])

    def share_dosages():
        @pl.when(r % 8 == c)
        def _():
            zc_own.start()
            for n in range(15):
                zcs[n].start()

    for i in range(8):
        @pl.when(r != i)
        def _():
            rdma(zpb.at[i], zpb.at[i], zp_send.at[0], zp_recv.at[i], (r, sib)).wait_recv()
    zp = jnp.concatenate([zpb[i] for i in range(8)], axis=1)

    early = [
        (lambda: e2(1), lambda: e1(2), lambda: e0(3)),
        (lambda: e0(5), lambda: e2(3), own_rows, lambda: e0(8)),
        (lambda: e0(7), lambda: e2(4)),
        (lambda: e2(5),),
        (lambda: e2(6), lambda: e1(8)),
        (lambda: e2(7),),
        (lambda: e2(8),),
        (),
    ]
    late = [
        (lambda: e0(4), lambda: e2(2), lambda: e1(3), share_dosages, lambda: r1(0)),
        (lambda: e0(6), lambda: e1(4), lambda: r1(1)),
        (lambda: e1(5), lambda: r2(0)),
        (lambda: e1(6), lambda: r2(1)),
        (lambda: e1(7), lambda: r3(0)),
        (lambda: r3(1),),
        (lambda: r4(0),),
        (lambda: r4(1),),
    ]

    def prepare(k):
        kb = k * NB
        n = BOTH - kb
        s = lax.dot_general(zp[:, kb : kb + NB], zp[:, kb:], TN, preferred_element_type=F32)
        g = jnp.concatenate([ps[k, j] for j in range(k, 8)], axis=1)
        on = lax.broadcasted_iota(jnp.int32, (NB, n), 0) == lax.broadcasted_iota(jnp.int32, (NB, n), 1)
        a = gv * (g + swn * s) + jnp.where(on, nv, 0.0)
        if k > 0:
            a = a + v_ref[kb : kb + NB, kb:]
        v_ref[kb : kb + NB, kb:] = a
        dbuf[...] = a[:, :NB]

    e1(0)
    e0(1)
    e2(0)
    e0(2)
    e1(1)
    e3(0)
    prepare(0)
    r0()

    @pl.loop(0, 8)
    def _(k):
        slabs = [dbuf[8 * s : 8 * s + 8, :] for s in range(16)]
        for s, v in enumerate(inverse_factor_128(slabs)):
            vkb[8 * s : 8 * s + 8, :] = v
        for kk in range(8):
            @pl.when(k == kk)
            def _():
                kb = kk * NB
                for f in early[kk]:
                    f()
                vk = vkb[...]
                parts = []
                if kk > 0:
                    parts.append(dot3(*split(vk), *split(v_ref[kb : kb + NB, :kb]), NN))
                parts.append(vk)
                if kk < 7:
                    right = dot3(*split(vk), *split(v_ref[kb : kb + NB, kb + NB :]), NN)
                    parts.append(right)
                    u = jnp.concatenate(parts, axis=1)
                    upd = dot3(*split(right), *split(u), TN)
                    if kk > 0:
                        v_ref[kb + NB :, :kb] = v_ref[kb + NB :, :kb] - upd[:, :kb]
                        v_ref[kb : kb + NB, :kb] = parts[0]
                        v_ref[kb + NB :, kb + NB :] = v_ref[kb + NB :, kb + NB :] - upd[:, kb + NB :]
                    else:
                        v_ref[kb + NB :, kb + NB :] = -upd[:, kb + NB :]
                    v_ref[kb + NB :, kb : kb + NB] = -upd[:, kb : kb + NB]
                    v_ref[kb : kb + NB, kb : kb + NB] = vk
                    v_ref[kb : kb + NB, kb + NB :] = jnp.zeros((NB, BOTH - kb - NB), F32)
                else:
                    v_ref[kb : kb + NB, :] = jnp.concatenate(parts, axis=1)
                for f in late[kk]:
                    f()
                if kk + 1 < 8:
                    e3(kk + 1)
                    prepare(kk + 1)

    e3(8)
    for J in range(4):
        js = slice(J * 256, (J + 1) * 256)
        h, lo = split(v_ref[js, :])
        vh[js, :] = h
        vl[js, :] = lo

    @pl.loop(0, 8)
    def _(rb):
        rows = pl.ds(pl.multiple_of(rb * NB, NB), NB)
        s = lax.dot_general(zr_ref[:, rows], jnp.concatenate([zpb[i] for i in range(8)], axis=1), TN, preferred_element_type=F32)
        r_at = lax.broadcasted_iota(jnp.int32, (NB, BOTH), 0) + (r + 16 * rb) * NB
        c_at = lax.broadcasted_iota(jnp.int32, (NB, BOTH), 1)
        a = gv * (jnp.concatenate([lbuf[k, rows, :] for k in range(8)], axis=1) + swn * s) + jnp.where(r_at == c_at, nv, 0.0)
        h, lo = split(a)
        ah[rows, :] = h
        al[rows, :] = lo

    for J in range(4):
        K = (J + 1) * 256
        js = slice(J * 256, (J + 1) * 256)
        abuf[:, js] = dot3(ah[:, :K], al[:, :K], vh[js, :K], vl[js, :K], NT)

    keep1 = jnp.where(r >= 4, 1.0, 0.0)
    keep2 = jnp.where(r >= 8, 1.0, 0.0)
    for rb in range(8):
        rows = slice(rb * NB, (rb + 1) * NB)
        a = abuf[rows, :]
        if rb == 0:
            c_at = lax.broadcasted_iota(jnp.int32, (NB, BOTH), 1)
            a = a * jnp.where(c_at < PANEL, keep1, keep2)
        h, lo = split(a)
        ah[rows, :] = h
        al[rows, :] = lo

    for J in range(4):
        js = slice(J * 256, (J + 1) * 256)
        K = slice(J * 256, BOTH)
        h, lo = split(dot3(ah[:, K], al[:, K], vh[K, js], vl[K, js], NN))
        wh[:, js] = h
        wl[:, js] = lo

    for hh in range(2):
        @pl.when(r != c + 8 * hh)
        def _():
            rdma(zr_ref, zcb.at[hh], zc_send.at[0], zc_recv.at[hh], (r, sib)).wait_recv()

    @pl.when(r % 8 == c)
    def _():
        zc_own.wait()

    r2v = rbuf.reshape(16384, NB)
    zr = zr_ref[...]
    eye = jnp.where(
        lax.broadcasted_iota(jnp.int32, (NB, NB), 0) == lax.broadcasted_iota(jnp.int32, (NB, NB), 1), nv, 0.0
    )
    stores = [
        pltpu.make_async_copy(gbuf.at[:, 8 * h : 8 * h + 8], out_hbm.at[:, 8 * h : 8 * h + 8], loc.at[h])
        for h in range(2)
    ]
    for half in range(2):
        r5(half)

        @pl.loop(4 * half, 4 * half + 4)
        def _(p):
            where = pl.ds(pl.multiple_of(p * NB, NB), NB)
            zc = jnp.concatenate([zcb[0, :, where], zcb[1, :, where]], axis=1)
            s = lax.dot_general(zp, zc, TN, preferred_element_type=F32)
            for e in range(2):
                es = slice(e * NB, (e + 1) * NB)
                raw = r2v[pl.ds(2 * p + e, BOTH, stride=16), :]
                hi, lo = split(gv * (raw + swn * s[:, es]))
                rh[:, es] = hi
                rl[:, es] = lo
            ub[...] = dot3(wh[...], wl[...], rh[...], rl[...], NN)
            own = lax.dot_general(zr, zc, TN, preferred_element_type=F32)
            for rb in range(8):
                rows = slice(rb * NB, (rb + 1) * NB)
                for e in range(2):
                    es = slice(e * NB, (e + 1) * NB)
                    lc = 2 * p + e
                    place = pl.ds(rb * 2048 + lc, NB, stride=16)
                    on = jnp.where(16 * rb + r == 8 * lc + c, 1.0, 0.0)
                    g2[place, :] = gv * (g2[place, :] + swn * own[rows, es]) - ub[rows, es] + on * eye

        if half == 0:
            mine = pl.ds(pl.multiple_of(c * NB, NB), NB)
            r_at = lax.broadcasted_iota(jnp.int32, (NB, NB), 0) + r * NB
            c_at = lax.broadcasted_iota(jnp.int32, (NB, NB), 1) + c * NB
            for rb in range(8):
                a = abuf[rb * NB : (rb + 1) * NB, mine]
                if rb == 0:
                    a = jnp.where(r_at >= c_at, a, 0.0)
                g2[pl.ds(rb * 2048, NB, stride=16), :] = a
        stores[half].start()
    for d in stores:
        d.wait()

    @pl.when(r < 8)
    def _():
        for n in range(15):
            xz[n].wait_send()
            zps[n].wait_send()

    @pl.when(r % 8 == c)
    def _():
        for n in range(15):
            zcs[n].wait_send()

    for i in range(ITEMS):
        for name in items[i]:
            items[i][name].wait_send()
    for h in range(2):
        @pl.when(x < 2)
        def _():
            Q[h]["far"].wait_send()
        for name in ("mate", "fu", "fd", "su", "sd", "ff", "sf"):
            Q[h][name].wait_send()


def factored(scal, zr, g):
    hbm = pl.BlockSpec(memory_space=pl.ANY)
    vmem = pl.BlockSpec(memory_space=pltpu.VMEM)
    dma = pltpu.SemaphoreType.DMA
    return pl.pallas_call(
        panel_kernel,
        out_shape=jax.ShapeDtypeStruct((1024, 16, NB), F32),
        in_specs=[pl.BlockSpec(memory_space=pltpu.SMEM)] * 3 + [vmem, hbm],
        out_specs=hbm,
        scratch_shapes=[
            pltpu.VMEM((BOTH, BOTH), F32),
            pltpu.VMEM((8, 8, NB, NB), F32),
            pltpu.VMEM((1024, 16, NB), F32),
            pltpu.VMEM((1024, NB), F32),
            pltpu.VMEM((8, MS, NB), BF16),
            pltpu.VMEM((2, MS, 1024), BF16),
            pltpu.VMEM((NB, NB), F32),
            pltpu.VMEM((NB, NB), F32),
            pltpu.VMEM((8, 1024, NB), F32),
            pltpu.VMEM((8, NB, 16, NB), F32),
            pltpu.VMEM((1024, BOTH), F32),
            pltpu.VMEM((1024, BOTH), BF16),
            pltpu.VMEM((1024, BOTH), BF16),
            pltpu.VMEM((BOTH, BOTH), BF16),
            pltpu.VMEM((BOTH, BOTH), BF16),
            pltpu.VMEM((1024, BOTH), BF16),
            pltpu.VMEM((1024, BOTH), BF16),
            pltpu.VMEM((BOTH, 256), BF16),
            pltpu.VMEM((BOTH, 256), BF16),
            pltpu.VMEM((1024, 256), F32),
            dma((15,)), dma((8,)), dma((15,)), dma((8,)), dma((15,)), dma((2,)),
            dma((ITEMS, 7)), dma((ITEMS, 7)), dma((8, 2)), dma((8, 2)), dma((5,)),
        ],
        compiler_params=pltpu.CompilerParams(
            vmem_limit_bytes=62 * 1024 * 1024, collective_id=0, has_side_effects=True
        ),
        cost_estimate=pl.CostEstimate(flops=45_000_000_000, bytes_accessed=18_000_000, transcendentals=0),
        name="panel_factor",
    )(*scal, zr, g)


def per_device(grm, dosages, slab_weight, genetic_var, noise_var):
    scal = (genetic_var, slab_weight, noise_var)
    return factored(scal, dosages.reshape(MS, 1024), grm.reshape(1024, 16, NB)).reshape(grm.shape)


def solution(mesh):
    in_specs = (P(None, "row", None, "col"), P(None, None, "row"), P(), P(), P())
    out_specs = P(None, "row", None, "col")
    return jax.shard_map(
        per_device, mesh=mesh, in_specs=in_specs, out_specs=out_specs, check_vma=False
    )
```

```python
import functools

import jax
import jax.numpy as jnp
from jax import lax
from jax.experimental import pallas as pl
from jax.experimental.pallas import tpu as pltpu
from jax.sharding import PartitionSpec as P

NB = 128
MS = 64
PANEL = 512
BOTH = 1024
F32 = jnp.float32
BF16 = jnp.bfloat16


def lane_bcast(x, j):
    return jnp.broadcast_to(x[:, j : j + 1], (8, 128))


def sub_bcast(x, i):
    return jnp.broadcast_to(x[i : i + 1, :], (8, 128))


def inverse_factor_128(slabs):
    lane = lax.broadcasted_iota(jnp.int32, (8, 128), 1)
    sub = lax.broadcasted_iota(jnp.int32, (8, 128), 0)
    slabs = list(slabs)
    for s in range(16):
        cols = {t: [lane_bcast(slabs[t], 8 * s + k) for k in range(8)] for t in range(s, 16)}
        b = {(i, k): sub_bcast(cols[s][k], i) for k in range(8) for i in range(k, 8)}
        here = (lane >= 8 * s) & (lane < 8 * s + 8)
        ident = (lane - 8 * s == sub).astype(F32)
        rp = jnp.where(here, ident, slabs[s])
        r = [sub_bcast(rp, i) for i in range(8)]
        inv = [None] * 8
        l = {}
        if s < 15:
            nx = jnp.where(here, 0.0, slabs[s + 1])
            cn = list(cols[s + 1])
        for j in range(0, 8, 2):
            a, e, f = b[j, j], b[j + 1, j], b[j + 1, j + 1]
            rd = 1.0 / (a * f - e * e)
            inv[j] = 1.0 / a
            l[j + 1, j] = e * inv[j]
            inv[j + 1] = a * rd
            m0, m1 = {}, {}
            for i in range(j + 2, 8):
                m0[i] = (b[i, j] * f - b[i, j + 1] * e) * rd
                m1[i] = (b[i, j + 1] * a - b[i, j] * e) * rd
                l[i, j] = b[i, j] * inv[j]
                l[i, j + 1] = m1[i]
            for i in range(j + 2, 8):
                for m in range(j + 2, i + 1):
                    b[i, m] = b[i, m] - (m0[i] * b[m, j] + m1[i] * b[m, j + 1])
            for i in range(j + 2, 8):
                r[i] = r[i] - (m0[i] * r[j] + m1[i] * r[j + 1])
            if s < 15:
                q0 = (cn[j] * f - cn[j + 1] * e) * rd
                q1 = (cn[j + 1] * a - cn[j] * e) * rd
                nx = nx - (q0 * r[j] + q1 * r[j + 1])
                for i in range(j + 2, 8):
                    cn[i] = cn[i] - (m0[i] * cn[j] + m1[i] * cn[j + 1])
            r[j + 1] = r[j + 1] - l[j + 1, j] * r[j]
            b[j + 1, j + 1] = f - l[j + 1, j] * e
        out = None
        for i in range(8):
            v = r[i] * lax.rsqrt(b[i, i])
            out = v if out is None else jnp.where(sub == i, v, out)
        w = [r[i] * inv[i] for i in range(8)]
        for j in range(7, 0, -1):
            for i in range(j):
                w[i] = w[i] - l[j, i] * w[j]
        slabs[s] = jnp.where(lane < 8 * s + 8, out, 0.0)
        if s < 15:
            slabs[s + 1] = nx
        for t in range(s + 2, 16):
            acc = cols[t][0] * w[0]
            for k in range(1, 8):
                acc = acc + cols[t][k] * w[k]
            slabs[t] = jnp.where(here, 0.0, slabs[t]) - acc
    return slabs


NN = (((1,), (0,)), ((), ()))
NT = (((1,), (1,)), ((), ()))
TN = (((0,), (0,)), ((), ()))
MESH = pl.DeviceIdType.MESH
ITEMS = 9


def split(x):
    hi = x.astype(BF16)
    return hi, (x - hi.astype(F32)).astype(BF16)


def dot3(ah, al, bh, bl, dims):
    d = functools.partial(lax.dot_general, dimension_numbers=dims, preferred_element_type=F32)
    return d(ah, bh) + (d(ah, bl) + d(al, bh))


def panel_kernel(
    gv_ref, sw_ref, nv_ref, zr_ref, g_hbm,
    out_hbm,
    v_ref, ps, gbuf, blk, zpb, zcb, dbuf, vkb, lbuf, rbuf, abuf, ah, al, vh, vl, wh, wl, rh, rl, ub,
    xz_send, xz_recv, zp_send, zp_recv, zc_send, zc_recv, c_send, c_recv, q_send, q_recv, loc,
):
    gv, sw, nv = gv_ref[0], sw_ref[0], nv_ref[0]
    swn = sw / MS
    r = lax.axis_index("row")
    c = lax.axis_index("col")
    x, z = r // 4, r % 4
    core = c % 2

    barrier = pltpu.get_barrier_semaphore()
    for o in range(1, 16):
        pl.semaphore_signal(barrier, inc=1, device_id=((r + o) % 16, c), device_id_type=MESH)
    for o in range(1, 8):
        pl.semaphore_signal(barrier, inc=1, device_id=(r, (c + o) % 8), device_id_type=MESH)

    first = pltpu.make_async_copy(g_hbm.at[0:128], gbuf.at[0:128], loc.at[0])
    rest = pltpu.make_async_copy(g_hbm.at[128:1024], gbuf.at[128:1024], loc.at[1])
    first.start()
    slab_copy = pltpu.make_async_copy(g_hbm.at[0:128], rbuf.at[r % 8], loc.at[2])

    g2 = gbuf.reshape(16384, NB)
    first.wait()
    rest.start()

    @pl.when(r < 8)
    def _():
        slab_copy.start()

    blk[0:NB, :] = g2[pl.ds(0, NB, stride=16), :]

    @pl.when(r < 8)
    def _():
        ps[r % 8, c] = blk[0:NB, :]
        zpb[r % 8] = zr_ref[:, 0:NB]

    pl.semaphore_wait(barrier, 22)

    def rdma(src, dst, ssem, rsem, to):
        return pltpu.make_async_remote_copy(
            src_ref=src, dst_ref=dst, send_sem=ssem, recv_sem=rsem, device_id=to, device_id_type=MESH
        )

    rs = r % 8
    xz, zps, zcs = [], [], []
    for n, o in enumerate((8, 4, 12, 2, 6, 10, 14, 1, 3, 5, 7, 9, 11, 13, 15)):
        to = ((r + o) % 16, c)
        xz.append(rdma(ps.at[rs, c], ps.at[rs, c], xz_send.at[n], xz_recv.at[rs], to))
        zps.append(rdma(zpb.at[rs], zpb.at[rs], zp_send.at[n], zp_recv.at[rs], to))
        zcs.append(rdma(zr_ref, zcb.at[r // 8], zc_send.at[n], zc_recv.at[r // 8], to))

    @pl.when(r < 3)
    def _():
        for n in range(15):
            xz[n].start()

    @pl.when(r < 8)
    def _():
        for n in range(15):
            zps[n].start()

    def own_rows():
        rest.wait()
        for rb in range(1, 8):
            blk[rb * NB : (rb + 1) * NB, :] = g2[pl.ds(rb * 2048, NB, stride=16), :]
        lbuf[c] = blk[...]

    cp, cm, co, sib = (c + 2) % 8, (c + 6) % 8, (c + 4) % 8, c + 1 - 2 * core
    fwd_src = jnp.where(core == 0, cm, cp)
    fwd_to = jnp.where(core == 0, cp, cm)

    def at(i, k):
        return ps.at[i, k] if i < 8 else lbuf.at[k]

    def gather(i):
        me = lambda k: at(i, k)
        own = blk if i == 8 else me(c)
        return dict(
            plus=rdma(own, me(c), c_send.at[i, 0], c_recv.at[i, 0], (r, cp)),
            minus=rdma(own, me(c), c_send.at[i, 1], c_recv.at[i, 1], (r, cm)),
            fwd=rdma(me(fwd_src), me(fwd_src), c_send.at[i, 2], c_recv.at[i, 2], (r, fwd_to)),
            s0=rdma(own, me(c), c_send.at[i, 3], c_recv.at[i, 3], (r, sib)),
            s1=rdma(me(cm), me(cm), c_send.at[i, 4], c_recv.at[i, 4], (r, sib)),
            s2=rdma(me(cp), me(cp), c_send.at[i, 5], c_recv.at[i, 5], (r, sib)),
            s3=rdma(me(co), me(co), c_send.at[i, 6], c_recv.at[i, 6], (r, sib)),
        )

    items = [gather(i) for i in range(ITEMS)]

    def e0(i):
        if i < 8:
            @pl.when(r != i)
            def _():
                rdma(ps.at[i, c], ps.at[i, c], xz_send.at[0], xz_recv.at[i], (r, sib)).wait_recv()
        for name in ("plus", "minus", "s0"):
            items[i][name].start()

    def e1(i):
        items[i]["plus"].wait_recv()
        items[i]["minus"].wait_recv()
        for name in ("fwd", "s1", "s2"):
            items[i][name].start()

    def e2(i):
        items[i]["fwd"].wait_recv()
        items[i]["s3"].start()

    def e3(i):
        for name in ("s0", "s1", "s2", "s3"):
            items[i][name].wait_recv()

    fs = jnp.where((x == 0) | (x == 3), 0, 1)
    up, down = x * 4 + (z + 1) % 4, x * 4 + (z + 3) % 4
    far = (3 - x) * 4 + z
    partner = (x + 1 - 2 * (x % 2)) * 4 + z

    def part(which, dz, h):
        s = 4 * (fs if which == 0 else 1 - fs) + (z + dz) % 4
        return rbuf.at[s, :, 8 * h : 8 * h + 8]

    def q(n, h, ref, to):
        return rdma(ref, ref, q_send.at[n, h], q_recv.at[n, h], (to, c))

    Q = []
    for h in range(2):
        f_src = jnp.where(core == 0, (z + 3) % 4, (z + 1) % 4)
        f_to = jnp.where(core == 0, up, down)
        Q.append(
            dict(
                far=q(0, h, part(0, 0, h), far),
                mate=q(1, h, part(0, 0, h), partner),
                fu=q(2, h, part(0, 0, h), up),
                fd=q(3, h, part(0, 0, h), down),
                su=q(4, h, part(1, 0, h), up),
                sd=q(5, h, part(1, 0, h), down),
                ff=q(6, h, rbuf.at[4 * fs + f_src, :, 8 * h : 8 * h + 8], f_to),
                xf=q(7, h, part(0, 2, h), partner),
            )
        )

    def r0(h):
        @pl.when(x < 2)
        def _():
            if h == 0:
                slab_copy.wait()
            Q[h]["far"].start()

    def r1a(h):
        @pl.when(x < 2)
        def _():
            spread(h)

    def spread(h):
        for name in ("mate", "fu", "fd"):
            Q[h][name].start()

    def r1(h):
        @pl.when(x >= 2)
        def _():
            Q[h]["far"].wait_recv()
            spread(h)

    def r2(h):
        Q[h]["mate"].wait_recv()
        Q[h]["su"].start()
        Q[h]["sd"].start()

    def r3(h):
        Q[h]["fu"].wait_recv()
        Q[h]["fd"].wait_recv()
        Q[h]["ff"].start()

    def r4(h):
        Q[h]["ff"].wait_recv()
        Q[h]["xf"].start()

    def r5(h):
        Q[h]["su"].wait_recv()
        Q[h]["sd"].wait_recv()
        Q[h]["xf"].wait_recv()

    r0(0)
    e0(0)

    @pl.when((r >= 3) & (r < 8))
    def _():
        for n in range(15):
            xz[n].start()

    r0(1)
    r1a(0)
    zc_own = pltpu.make_async_copy(zr_ref, zcb.at[r // 8], loc.at[4])

    def share_dosages():
        @pl.when(r % 8 == c)
        def _():
            zc_own.start()
            for n in range(15):
                zcs[n].start()

    for i in range(8):
        @pl.when(r != i)
        def _():
            rdma(zpb.at[i], zpb.at[i], zp_send.at[0], zp_recv.at[i], (r, sib)).wait_recv()
    zp = jnp.concatenate([zpb[i] for i in range(8)], axis=1)

    early = [
        (lambda: e2(1), lambda: e1(2), lambda: e0(3), lambda: r1(0)),
        (lambda: e0(5), lambda: e1(3)),
        (lambda: e0(7), lambda: e1(5)),
        (lambda: e1(6),),
        (),
        (),
        (),
        (),
    ]
    late = [
        (lambda: e0(4), lambda: e2(2), share_dosages, lambda: r1a(1)),
        (lambda: e0(6), lambda: e1(4), lambda: e2(3), lambda: r1(1)),
        (lambda: e2(4), lambda: r3(0), lambda: r2(0)),
        (lambda: e1(7), lambda: e2(5), own_rows, lambda: e0(8)),
        (lambda: e2(6), lambda: r3(1), lambda: r2(1)),
        (lambda: e2(7), lambda: e1(8)),
        (lambda: e2(8), lambda: r4(0)),
        (),
    ]

    def prepare(k):
        kb = k * NB
        n = BOTH - kb
        s = lax.dot_general(zp[:, kb : kb + NB], zp[:, kb:], TN, preferred_element_type=F32)
        g = jnp.concatenate([ps[k, j] for j in range(k, 8)], axis=1)
        on = lax.broadcasted_iota(jnp.int32, (NB, n), 0) == lax.broadcasted_iota(jnp.int32, (NB, n), 1)
        a = gv * (g + swn * s) + jnp.where(on, nv, 0.0)
        if k > 0:
            a = a + v_ref[kb : kb + NB, kb:]
        v_ref[kb : kb + NB, kb:] = a
        dbuf[...] = a[:, :NB]

    e1(0)
    e0(1)
    e2(0)
    e0(2)
    e1(1)
    e3(0)
    prepare(0)

    @pl.loop(0, 8)
    def _(k):
        slabs = [dbuf[8 * s : 8 * s + 8, :] for s in range(16)]
        for s, v in enumerate(inverse_factor_128(slabs)):
            vkb[8 * s : 8 * s + 8, :] = v
        for kk in range(8):
            @pl.when(k == kk)
            def _():
                kb = kk * NB
                for f in early[kk]:
                    f()
                vk = vkb[...]
                parts = []
                if kk > 0:
                    parts.append(dot3(*split(vk), *split(v_ref[kb : kb + NB, :kb]), NN))
                parts.append(vk)
                if kk < 7:
                    right = dot3(*split(vk), *split(v_ref[kb : kb + NB, kb + NB :]), NN)
                    parts.append(right)
                    u = jnp.concatenate(parts, axis=1)
                    upd = dot3(*split(right), *split(u), TN)
                    if kk > 0:
                        v_ref[kb + NB :, :kb] = v_ref[kb + NB :, :kb] - upd[:, :kb]
                        v_ref[kb : kb + NB, :kb] = parts[0]
                        v_ref[kb + NB :, kb + NB :] = v_ref[kb + NB :, kb + NB :] - upd[:, kb + NB :]
                    else:
                        v_ref[kb + NB :, kb + NB :] = -upd[:, kb + NB :]
                    v_ref[kb + NB :, kb : kb + NB] = -upd[:, kb : kb + NB]
                    v_ref[kb : kb + NB, kb : kb + NB] = vk
                    v_ref[kb : kb + NB, kb + NB :] = jnp.zeros((NB, BOTH - kb - NB), F32)
                else:
                    v_ref[kb : kb + NB, :] = jnp.concatenate(parts, axis=1)
                for f in late[kk]:
                    f()
                if kk + 1 < 8:
                    e3(kk + 1)
                    prepare(kk + 1)

    e3(8)
    for J in range(4):
        js = slice(J * 256, (J + 1) * 256)
        h, lo = split(v_ref[js, :])
        vh[js, :] = h
        vl[js, :] = lo

    @pl.loop(0, 8)
    def _(rb):
        rows = pl.ds(pl.multiple_of(rb * NB, NB), NB)
        s = lax.dot_general(zr_ref[:, rows], jnp.concatenate([zpb[i] for i in range(8)], axis=1), TN, preferred_element_type=F32)
        r_at = lax.broadcasted_iota(jnp.int32, (NB, BOTH), 0) + (r + 16 * rb) * NB
        c_at = lax.broadcasted_iota(jnp.int32, (NB, BOTH), 1)
        a = gv * (jnp.concatenate([lbuf[k, rows, :] for k in range(8)], axis=1) + swn * s) + jnp.where(r_at == c_at, nv, 0.0)
        h, lo = split(a)
        ah[rows, :] = h
        al[rows, :] = lo

    for J in range(4):
        K = (J + 1) * 256
        js = slice(J * 256, (J + 1) * 256)
        abuf[:, js] = dot3(ah[:, :K], al[:, :K], vh[js, :K], vl[js, :K], NT)

    r4(1)

    keep1 = jnp.where(r >= 4, 1.0, 0.0)
    keep2 = jnp.where(r >= 8, 1.0, 0.0)
    for rb in range(8):
        rows = slice(rb * NB, (rb + 1) * NB)
        a = abuf[rows, :]
        if rb == 0:
            c_at = lax.broadcasted_iota(jnp.int32, (NB, BOTH), 1)
            a = a * jnp.where(c_at < PANEL, keep1, keep2)
        h, lo = split(a)
        ah[rows, :] = h
        al[rows, :] = lo

    for J in range(4):
        js = slice(J * 256, (J + 1) * 256)
        K = slice(J * 256, BOTH)
        h, lo = split(dot3(ah[:, K], al[:, K], vh[K, js], vl[K, js], NN))
        wh[:, js] = h
        wl[:, js] = lo

    for hh in range(2):
        @pl.when(r != c + 8 * hh)
        def _():
            rdma(zr_ref, zcb.at[hh], zc_send.at[0], zc_recv.at[hh], (r, sib)).wait_recv()

    @pl.when(r % 8 == c)
    def _():
        zc_own.wait()

    r2v = rbuf.reshape(16384, NB)
    zr = zr_ref[...]
    eye = jnp.where(
        lax.broadcasted_iota(jnp.int32, (NB, NB), 0) == lax.broadcasted_iota(jnp.int32, (NB, NB), 1), nv, 0.0
    )
    stores = [
        pltpu.make_async_copy(gbuf.at[:, 8 * h : 8 * h + 8], out_hbm.at[:, 8 * h : 8 * h + 8], loc.at[h])
        for h in range(2)
    ]
    for half in range(2):
        r5(half)

        @pl.loop(4 * half, 4 * half + 4)
        def _(p):
            where = pl.ds(pl.multiple_of(p * NB, NB), NB)
            zc = jnp.concatenate([zcb[0, :, where], zcb[1, :, where]], axis=1)
            s = lax.dot_general(zp, zc, TN, preferred_element_type=F32)
            for e in range(2):
                es = slice(e * NB, (e + 1) * NB)
                raw = r2v[pl.ds(2 * p + e, BOTH, stride=16), :]
                hi, lo = split(gv * (raw + swn * s[:, es]))
                rh[:, es] = hi
                rl[:, es] = lo
            ub[...] = dot3(wh[...], wl[...], rh[...], rl[...], NN)
            own = lax.dot_general(zr, zc, TN, preferred_element_type=F32)
            for rb in range(8):
                rows = slice(rb * NB, (rb + 1) * NB)
                for e in range(2):
                    es = slice(e * NB, (e + 1) * NB)
                    lc = 2 * p + e
                    place = pl.ds(rb * 2048 + lc, NB, stride=16)
                    on = jnp.where(16 * rb + r == 8 * lc + c, 1.0, 0.0)
                    g2[place, :] = gv * (g2[place, :] + swn * own[rows, es]) - ub[rows, es] + on * eye

        if half == 0:
            mine = pl.ds(pl.multiple_of(c * NB, NB), NB)
            r_at = lax.broadcasted_iota(jnp.int32, (NB, NB), 0) + r * NB
            c_at = lax.broadcasted_iota(jnp.int32, (NB, NB), 1) + c * NB
            for rb in range(8):
                a = abuf[rb * NB : (rb + 1) * NB, mine]
                if rb == 0:
                    a = jnp.where(r_at >= c_at, a, 0.0)
                g2[pl.ds(rb * 2048, NB, stride=16), :] = a
        stores[half].start()
    for d in stores:
        d.wait()

    @pl.when(r < 8)
    def _():
        for n in range(15):
            xz[n].wait_send()
            zps[n].wait_send()

    @pl.when(r % 8 == c)
    def _():
        for n in range(15):
            zcs[n].wait_send()

    for i in range(ITEMS):
        for name in items[i]:
            items[i][name].wait_send()
    for h in range(2):
        @pl.when(x < 2)
        def _():
            Q[h]["far"].wait_send()
        for name in ("mate", "fu", "fd", "su", "sd", "ff", "xf"):
            Q[h][name].wait_send()


def factored(scal, zr, g):
    hbm = pl.BlockSpec(memory_space=pl.ANY)
    vmem = pl.BlockSpec(memory_space=pltpu.VMEM)
    dma = pltpu.SemaphoreType.DMA
    return pl.pallas_call(
        panel_kernel,
        out_shape=jax.ShapeDtypeStruct((1024, 16, NB), F32),
        in_specs=[pl.BlockSpec(memory_space=pltpu.SMEM)] * 3 + [vmem, hbm],
        out_specs=hbm,
        scratch_shapes=[
            pltpu.VMEM((BOTH, BOTH), F32),
            pltpu.VMEM((8, 8, NB, NB), F32),
            pltpu.VMEM((1024, 16, NB), F32),
            pltpu.VMEM((1024, NB), F32),
            pltpu.VMEM((8, MS, NB), BF16),
            pltpu.VMEM((2, MS, 1024), BF16),
            pltpu.VMEM((NB, NB), F32),
            pltpu.VMEM((NB, NB), F32),
            pltpu.VMEM((8, 1024, NB), F32),
            pltpu.VMEM((8, NB, 16, NB), F32),
            pltpu.VMEM((1024, BOTH), F32),
            pltpu.VMEM((1024, BOTH), BF16),
            pltpu.VMEM((1024, BOTH), BF16),
            pltpu.VMEM((BOTH, BOTH), BF16),
            pltpu.VMEM((BOTH, BOTH), BF16),
            pltpu.VMEM((1024, BOTH), BF16),
            pltpu.VMEM((1024, BOTH), BF16),
            pltpu.VMEM((BOTH, 256), BF16),
            pltpu.VMEM((BOTH, 256), BF16),
            pltpu.VMEM((1024, 256), F32),
            dma((15,)), dma((8,)), dma((15,)), dma((8,)), dma((15,)), dma((2,)),
            dma((ITEMS, 7)), dma((ITEMS, 7)), dma((8, 2)), dma((8, 2)), dma((5,)),
        ],
        compiler_params=pltpu.CompilerParams(
            vmem_limit_bytes=62 * 1024 * 1024, collective_id=0, has_side_effects=True
        ),
        cost_estimate=pl.CostEstimate(flops=45_000_000_000, bytes_accessed=18_000_000, transcendentals=0),
        name="panel_factor",
    )(*scal, zr, g)


def per_device(grm, dosages, slab_weight, genetic_var, noise_var):
    scal = (genetic_var, slab_weight, noise_var)
    return factored(scal, dosages.reshape(MS, 1024), grm.reshape(1024, 16, NB)).reshape(grm.shape)


def solution(mesh):
    in_specs = (P(None, "row", None, "col"), P(None, None, "row"), P(), P(), P())
    out_specs = P(None, "row", None, "col")
    return jax.shard_map(
        per_device, mesh=mesh, in_specs=in_specs, out_specs=out_specs, check_vma=False
    )
```

```python
import functools

import jax
import jax.numpy as jnp
from jax import lax
from jax.experimental import pallas as pl
from jax.experimental.pallas import tpu as pltpu
from jax.sharding import PartitionSpec as P

NB = 128
MS = 64
PANEL = 512
BOTH = 1024
F32 = jnp.float32
BF16 = jnp.bfloat16


def lane_bcast(x, j):
    return jnp.broadcast_to(x[:, j : j + 1], (8, 128))


def sub_bcast(x, i):
    return jnp.broadcast_to(x[i : i + 1, :], (8, 128))


def inverse_factor_128(slabs):
    lane = lax.broadcasted_iota(jnp.int32, (8, 128), 1)
    sub = lax.broadcasted_iota(jnp.int32, (8, 128), 0)
    slabs = list(slabs)
    for s in range(16):
        cols = {t: [lane_bcast(slabs[t], 8 * s + k) for k in range(8)] for t in range(s, 16)}
        b = {(i, k): sub_bcast(cols[s][k], i) for k in range(8) for i in range(k, 8)}
        here = (lane >= 8 * s) & (lane < 8 * s + 8)
        ident = (lane - 8 * s == sub).astype(F32)
        rp = jnp.where(here, ident, slabs[s])
        r = [sub_bcast(rp, i) for i in range(8)]
        inv = [None] * 8
        l = {}
        if s < 15:
            nx = jnp.where(here, 0.0, slabs[s + 1])
            cn = list(cols[s + 1])
        for j in range(0, 8, 2):
            a, e, f = b[j, j], b[j + 1, j], b[j + 1, j + 1]
            rd = 1.0 / (a * f - e * e)
            inv[j] = 1.0 / a
            l[j + 1, j] = e * inv[j]
            inv[j + 1] = a * rd
            m0, m1 = {}, {}
            for i in range(j + 2, 8):
                m0[i] = (b[i, j] * f - b[i, j + 1] * e) * rd
                m1[i] = (b[i, j + 1] * a - b[i, j] * e) * rd
                l[i, j] = b[i, j] * inv[j]
                l[i, j + 1] = m1[i]
            for i in range(j + 2, 8):
                for m in range(j + 2, i + 1):
                    b[i, m] = b[i, m] - (m0[i] * b[m, j] + m1[i] * b[m, j + 1])
            for i in range(j + 2, 8):
                r[i] = r[i] - (m0[i] * r[j] + m1[i] * r[j + 1])
            if s < 15:
                q0 = (cn[j] * f - cn[j + 1] * e) * rd
                q1 = (cn[j + 1] * a - cn[j] * e) * rd
                nx = nx - (q0 * r[j] + q1 * r[j + 1])
                for i in range(j + 2, 8):
                    cn[i] = cn[i] - (m0[i] * cn[j] + m1[i] * cn[j + 1])
            r[j + 1] = r[j + 1] - l[j + 1, j] * r[j]
            b[j + 1, j + 1] = f - l[j + 1, j] * e
        out = None
        for i in range(8):
            v = r[i] * lax.rsqrt(b[i, i])
            out = v if out is None else jnp.where(sub == i, v, out)
        w = [r[i] * inv[i] for i in range(8)]
        for j in range(7, 0, -1):
            for i in range(j):
                w[i] = w[i] - l[j, i] * w[j]
        slabs[s] = jnp.where(lane < 8 * s + 8, out, 0.0)
        if s < 15:
            slabs[s + 1] = nx
        for t in range(s + 2, 16):
            acc = cols[t][0] * w[0]
            for k in range(1, 8):
                acc = acc + cols[t][k] * w[k]
            slabs[t] = jnp.where(here, 0.0, slabs[t]) - acc
    return slabs


NN = (((1,), (0,)), ((), ()))
NT = (((1,), (1,)), ((), ()))
TN = (((0,), (0,)), ((), ()))
MESH = pl.DeviceIdType.MESH
ITEMS = 9


def split(x):
    hi = x.astype(BF16)
    return hi, (x - hi.astype(F32)).astype(BF16)


def dot3(ah, al, bh, bl, dims):
    d = functools.partial(lax.dot_general, dimension_numbers=dims, preferred_element_type=F32)
    return d(ah, bh) + (d(ah, bl) + d(al, bh))


def panel_kernel(
    gv_ref, sw_ref, nv_ref, zr_ref, g_hbm,
    out_hbm,
    v_ref, ps, gbuf, blk, zpb, zcb, dbuf, vkb, lbuf, rbuf, abuf, ah, al, vh, vl, wh, wl, rh, rl, ub,
    xz_send, xz_recv, zp_send, zp_recv, zc_send, zc_recv, c_send, c_recv, q_send, q_recv, loc,
):
    gv, sw, nv = gv_ref[0], sw_ref[0], nv_ref[0]
    swn = sw / MS
    r = lax.axis_index("row")
    c = lax.axis_index("col")
    x, z = r // 4, r % 4
    core = c % 2

    barrier = pltpu.get_barrier_semaphore()
    for o in range(1, 16):
        pl.semaphore_signal(barrier, inc=1, device_id=((r + o) % 16, c), device_id_type=MESH)
    for o in range(1, 8):
        pl.semaphore_signal(barrier, inc=1, device_id=(r, (c + o) % 8), device_id_type=MESH)

    first = pltpu.make_async_copy(g_hbm.at[0:128], gbuf.at[0:128], loc.at[0])
    rest = pltpu.make_async_copy(g_hbm.at[128:1024], gbuf.at[128:1024], loc.at[1])
    first.start()
    slab_copy = pltpu.make_async_copy(g_hbm.at[0:128], rbuf.at[r % 8], loc.at[2])

    g2 = gbuf.reshape(16384, NB)
    first.wait()
    rest.start()

    @pl.when(r < 8)
    def _():
        slab_copy.start()

    blk[0:NB, :] = g2[pl.ds(0, NB, stride=16), :]

    @pl.when(r < 8)
    def _():
        ps[r % 8, c] = blk[0:NB, :]
        zpb[r % 8] = zr_ref[:, 0:NB]

    pl.semaphore_wait(barrier, 22)

    def rdma(src, dst, ssem, rsem, to):
        return pltpu.make_async_remote_copy(
            src_ref=src, dst_ref=dst, send_sem=ssem, recv_sem=rsem, device_id=to, device_id_type=MESH
        )

    rs = r % 8
    xz, zps, zcs = [], [], []
    for n, o in enumerate((8, 4, 12, 2, 6, 10, 14, 1, 3, 5, 7, 9, 11, 13, 15)):
        to = ((r + o) % 16, c)
        xz.append(rdma(ps.at[rs, c], ps.at[rs, c], xz_send.at[n], xz_recv.at[rs], to))
        zps.append(rdma(zpb.at[rs], zpb.at[rs], zp_send.at[n], zp_recv.at[rs], to))
        zcs.append(rdma(zr_ref, zcb.at[r // 8], zc_send.at[n], zc_recv.at[r // 8], to))

    @pl.when(r < 3)
    def _():
        for n in range(15):
            xz[n].start()

    @pl.when(r < 8)
    def _():
        for n in range(15):
            zps[n].start()

    def own_rows():
        rest.wait()
        for rb in range(1, 8):
            blk[rb * NB : (rb + 1) * NB, :] = g2[pl.ds(rb * 2048, NB, stride=16), :]
        lbuf[c] = blk[...]

    cp, cm, co, sib = (c + 2) % 8, (c + 6) % 8, (c + 4) % 8, c + 1 - 2 * core
    fwd_src = jnp.where(core == 0, cm, cp)
    fwd_to = jnp.where(core == 0, cp, cm)

    def at(i, k):
        return ps.at[i, k] if i < 8 else lbuf.at[k]

    def gather(i):
        me = lambda k: at(i, k)
        own = blk if i == 8 else me(c)
        return dict(
            plus=rdma(own, me(c), c_send.at[i, 0], c_recv.at[i, 0], (r, cp)),
            minus=rdma(own, me(c), c_send.at[i, 1], c_recv.at[i, 1], (r, cm)),
            fwd=rdma(me(fwd_src), me(fwd_src), c_send.at[i, 2], c_recv.at[i, 2], (r, fwd_to)),
            s0=rdma(own, me(c), c_send.at[i, 3], c_recv.at[i, 3], (r, sib)),
            s1=rdma(me(cm), me(cm), c_send.at[i, 4], c_recv.at[i, 4], (r, sib)),
            s2=rdma(me(cp), me(cp), c_send.at[i, 5], c_recv.at[i, 5], (r, sib)),
            s3=rdma(me(co), me(co), c_send.at[i, 6], c_recv.at[i, 6], (r, sib)),
        )

    items = [gather(i) for i in range(ITEMS)]

    def e0(i):
        if i < 8:
            @pl.when(r != i)
            def _():
                rdma(ps.at[i, c], ps.at[i, c], xz_send.at[0], xz_recv.at[i], (r, sib)).wait_recv()
        for name in ("plus", "minus", "s0"):
            items[i][name].start()

    def e1(i):
        items[i]["plus"].wait_recv()
        items[i]["minus"].wait_recv()
        for name in ("fwd", "s1", "s2"):
            items[i][name].start()

    def e2(i):
        items[i]["fwd"].wait_recv()
        items[i]["s3"].start()

    def e3(i):
        for name in ("s0", "s1", "s2", "s3"):
            items[i][name].wait_recv()

    fs = jnp.where((x == 0) | (x == 3), 0, 1)
    up, down = x * 4 + (z + 1) % 4, x * 4 + (z + 3) % 4
    far = (3 - x) * 4 + z
    partner = (x + 1 - 2 * (x % 2)) * 4 + z

    def part(which, dz, h):
        s = 4 * (fs if which == 0 else 1 - fs) + (z + dz) % 4
        return rbuf.at[s, :, 8 * h : 8 * h + 8]

    def q(n, h, ref, to):
        return rdma(ref, ref, q_send.at[n, h], q_recv.at[n, h], (to, c))

    Q = []
    for h in range(2):
        f_src = jnp.where(core == 0, (z + 3) % 4, (z + 1) % 4)
        f_to = jnp.where(core == 0, up, down)
        Q.append(
            dict(
                far=q(0, h, part(0, 0, h), far),
                mate=q(1, h, part(0, 0, h), partner),
                fu=q(2, h, part(0, 0, h), up),
                fd=q(3, h, part(0, 0, h), down),
                su=q(4, h, part(1, 0, h), up),
                sd=q(5, h, part(1, 0, h), down),
                ff=q(6, h, rbuf.at[4 * fs + f_src, :, 8 * h : 8 * h + 8], f_to),
                xf=q(7, h, part(0, 2, h), partner),
            )
        )

    def r0(h):
        @pl.when(x < 2)
        def _():
            if h == 0:
                slab_copy.wait()
            Q[h]["far"].start()

    def r1a(h):
        @pl.when(x < 2)
        def _():
            spread(h)

    def spread(h):
        for name in ("mate", "fu", "fd"):
            Q[h][name].start()

    def r1(h):
        @pl.when(x >= 2)
        def _():
            Q[h]["far"].wait_recv()
            spread(h)

    def r2(h):
        Q[h]["mate"].wait_recv()
        Q[h]["su"].start()
        Q[h]["sd"].start()

    def r3(h):
        Q[h]["fu"].wait_recv()
        Q[h]["fd"].wait_recv()
        Q[h]["ff"].start()

    def r4(h):
        Q[h]["ff"].wait_recv()
        Q[h]["xf"].start()

    def r5(h):
        Q[h]["su"].wait_recv()
        Q[h]["sd"].wait_recv()
        Q[h]["xf"].wait_recv()

    r0(0)
    e0(0)

    @pl.when((r >= 3) & (r < 8))
    def _():
        for n in range(15):
            xz[n].start()

    r0(1)
    r1a(0)
    zc_own = pltpu.make_async_copy(zr_ref, zcb.at[r // 8], loc.at[4])

    def share_dosages():
        @pl.when(r % 8 == c)
        def _():
            zc_own.start()
            for n in range(15):
                zcs[n].start()

    for i in range(8):
        @pl.when(r != i)
        def _():
            rdma(zpb.at[i], zpb.at[i], zp_send.at[0], zp_recv.at[i], (r, sib)).wait_recv()
    zp = jnp.concatenate([zpb[i] for i in range(8)], axis=1)

    early = [
        (lambda: e2(1), lambda: e1(2), lambda: e0(3), lambda: r1(0)),
        (lambda: e0(5), lambda: e1(3)),
        (lambda: e0(7), lambda: e1(5)),
        (lambda: e1(6),),
        (),
        (),
        (),
        (),
    ]
    late = [
        (lambda: e0(4), lambda: e2(2), share_dosages, lambda: r1a(1)),
        (lambda: e0(6), lambda: e1(4), lambda: e2(3), lambda: r1(1)),
        (lambda: e2(4), lambda: r3(0), lambda: r2(0)),
        (lambda: e1(7), lambda: e2(5), own_rows, lambda: e0(8)),
        (lambda: e2(6), lambda: r3(1), lambda: r2(1)),
        (lambda: e2(7), lambda: e1(8)),
        (lambda: e2(8), lambda: r4(0)),
        (),
    ]

    def prepare(k):
        kb = k * NB
        n = BOTH - kb
        s = lax.dot_general(zp[:, kb : kb + NB], zp[:, kb:], TN, preferred_element_type=F32)
        g = jnp.concatenate([ps[k, j] for j in range(k, 8)], axis=1)
        on = lax.broadcasted_iota(jnp.int32, (NB, n), 0) == lax.broadcasted_iota(jnp.int32, (NB, n), 1)
        a = gv * (g + swn * s) + jnp.where(on, nv, 0.0)
        if k > 0:
            a = a + v_ref[kb : kb + NB, kb:]
        v_ref[kb : kb + NB, kb:] = a
        dbuf[...] = a[:, :NB]

    e1(0)
    e0(1)
    e2(0)
    e0(2)
    e1(1)
    e3(0)
    prepare(0)

    @pl.loop(0, 8)
    def _(k):
        slabs = [dbuf[8 * s : 8 * s + 8, :] for s in range(16)]
        for s, v in enumerate(inverse_factor_128(slabs)):
            vkb[8 * s : 8 * s + 8, :] = v
        for kk in range(8):
            @pl.when(k == kk)
            def _():
                kb = kk * NB
                for f in early[kk]:
                    f()
                vk = vkb[...]
                parts = []
                if kk > 0:
                    parts.append(dot3(*split(vk), *split(v_ref[kb : kb + NB, :kb]), NN))
                parts.append(vk)
                if kk < 7:
                    right = dot3(*split(vk), *split(v_ref[kb : kb + NB, kb + NB :]), NN)
                    parts.append(right)
                    u = jnp.concatenate(parts, axis=1)
                    upd = dot3(*split(right), *split(u), TN)
                    if kk > 0:
                        v_ref[kb + NB :, :kb] = v_ref[kb + NB :, :kb] - upd[:, :kb]
                        v_ref[kb : kb + NB, :kb] = parts[0]
                        v_ref[kb + NB :, kb + NB :] = v_ref[kb + NB :, kb + NB :] - upd[:, kb + NB :]
                    else:
                        v_ref[kb + NB :, kb + NB :] = -upd[:, kb + NB :]
                    v_ref[kb + NB :, kb : kb + NB] = -upd[:, kb : kb + NB]
                    v_ref[kb : kb + NB, kb : kb + NB] = vk
                    v_ref[kb : kb + NB, kb + NB :] = jnp.zeros((NB, BOTH - kb - NB), F32)
                else:
                    v_ref[kb : kb + NB, :] = jnp.concatenate(parts, axis=1)
                for f in late[kk]:
                    f()
                if kk + 1 < 8:
                    e3(kk + 1)
                    prepare(kk + 1)

    for J in range(4):
        js = slice(J * 256, (J + 1) * 256)
        h, lo = split(v_ref[js, :])
        vh[js, :] = h
        vl[js, :] = lo
    e3(8)

    @pl.loop(0, 8)
    def _(rb):
        rows = pl.ds(pl.multiple_of(rb * NB, NB), NB)
        s = lax.dot_general(zr_ref[:, rows], zp, TN, preferred_element_type=F32)
        r_at = lax.broadcasted_iota(jnp.int32, (NB, BOTH), 0) + (r + 16 * rb) * NB
        c_at = lax.broadcasted_iota(jnp.int32, (NB, BOTH), 1)
        a = gv * (jnp.concatenate([lbuf[k, rows, :] for k in range(8)], axis=1) + swn * s) + jnp.where(r_at == c_at, nv, 0.0)
        h, lo = split(a)
        ah[rows, :] = h
        al[rows, :] = lo

    for J in range(4):
        K = (J + 1) * 256
        js = slice(J * 256, (J + 1) * 256)
        abuf[:, js] = dot3(ah[:, :K], al[:, :K], vh[js, :K], vl[js, :K], NT)

    r4(1)

    keep1 = jnp.where(r >= 4, 1.0, 0.0)
    keep2 = jnp.where(r >= 8, 1.0, 0.0)
    for rb in range(8):
        rows = slice(rb * NB, (rb + 1) * NB)
        a = abuf[rows, :]
        if rb == 0:
            c_at = lax.broadcasted_iota(jnp.int32, (NB, BOTH), 1)
            a = a * jnp.where(c_at < PANEL, keep1, keep2)
        h, lo = split(a)
        ah[rows, :] = h
        al[rows, :] = lo

    for J in range(4):
        js = slice(J * 256, (J + 1) * 256)
        K = slice(J * 256, BOTH)
        h, lo = split(dot3(ah[:, K], al[:, K], vh[K, js], vl[K, js], NN))
        wh[:, js] = h
        wl[:, js] = lo

    for hh in range(2):
        @pl.when(r != c + 8 * hh)
        def _():
            rdma(zr_ref, zcb.at[hh], zc_send.at[0], zc_recv.at[hh], (r, sib)).wait_recv()

    @pl.when(r % 8 == c)
    def _():
        zc_own.wait()

    r2v = rbuf.reshape(16384, NB)
    zr = zr_ref[...]
    eye = jnp.where(
        lax.broadcasted_iota(jnp.int32, (NB, NB), 0) == lax.broadcasted_iota(jnp.int32, (NB, NB), 1), nv, 0.0
    )
    stores = [
        pltpu.make_async_copy(gbuf.at[:, 8 * h : 8 * h + 8], out_hbm.at[:, 8 * h : 8 * h + 8], loc.at[h])
        for h in range(2)
    ]
    for half in range(2):
        r5(half)

        @pl.loop(4 * half, 4 * half + 4)
        def _(p):
            where = pl.ds(pl.multiple_of(p * NB, NB), NB)
            zc = jnp.concatenate([zcb[0, :, where], zcb[1, :, where]], axis=1)
            s = lax.dot_general(zp, zc, TN, preferred_element_type=F32)
            for e in range(2):
                es = slice(e * NB, (e + 1) * NB)
                raw = r2v[pl.ds(2 * p + e, BOTH, stride=16), :]
                hi, lo = split(gv * (raw + swn * s[:, es]))
                rh[:, es] = hi
                rl[:, es] = lo
            ub[...] = dot3(wh[...], wl[...], rh[...], rl[...], NN)
            own = lax.dot_general(zr, zc, TN, preferred_element_type=F32)
            for rb in range(8):
                rows = slice(rb * NB, (rb + 1) * NB)
                for e in range(2):
                    es = slice(e * NB, (e + 1) * NB)
                    lc = 2 * p + e
                    place = pl.ds(rb * 2048 + lc, NB, stride=16)
                    on = jnp.where(16 * rb + r == 8 * lc + c, 1.0, 0.0)
                    g2[place, :] = gv * (g2[place, :] + swn * own[rows, es]) - ub[rows, es] + on * eye

        if half == 0:
            mine = pl.ds(pl.multiple_of(c * NB, NB), NB)
            r_at = lax.broadcasted_iota(jnp.int32, (NB, NB), 0) + r * NB
            c_at = lax.broadcasted_iota(jnp.int32, (NB, NB), 1) + c * NB
            for rb in range(8):
                a = abuf[rb * NB : (rb + 1) * NB, mine]
                if rb == 0:
                    a = jnp.where(r_at >= c_at, a, 0.0)
                g2[pl.ds(rb * 2048, NB, stride=16), :] = a
        stores[half].start()
    for d in stores:
        d.wait()

    @pl.when(r < 8)
    def _():
        for n in range(15):
            xz[n].wait_send()
            zps[n].wait_send()

    @pl.when(r % 8 == c)
    def _():
        for n in range(15):
            zcs[n].wait_send()

    for i in range(ITEMS):
        for name in items[i]:
            items[i][name].wait_send()
    for h in range(2):
        @pl.when(x < 2)
        def _():
            Q[h]["far"].wait_send()
        for name in ("mate", "fu", "fd", "su", "sd", "ff", "xf"):
            Q[h][name].wait_send()


def factored(scal, zr, g):
    hbm = pl.BlockSpec(memory_space=pl.ANY)
    vmem = pl.BlockSpec(memory_space=pltpu.VMEM)
    dma = pltpu.SemaphoreType.DMA
    return pl.pallas_call(
        panel_kernel,
        out_shape=jax.ShapeDtypeStruct((1024, 16, NB), F32),
        in_specs=[pl.BlockSpec(memory_space=pltpu.SMEM)] * 3 + [vmem, hbm],
        out_specs=hbm,
        scratch_shapes=[
            pltpu.VMEM((BOTH, BOTH), F32),
            pltpu.VMEM((8, 8, NB, NB), F32),
            pltpu.VMEM((1024, 16, NB), F32),
            pltpu.VMEM((1024, NB), F32),
            pltpu.VMEM((8, MS, NB), BF16),
            pltpu.VMEM((2, MS, 1024), BF16),
            pltpu.VMEM((NB, NB), F32),
            pltpu.VMEM((NB, NB), F32),
            pltpu.VMEM((8, 1024, NB), F32),
            pltpu.VMEM((8, NB, 16, NB), F32),
            pltpu.VMEM((1024, BOTH), F32),
            pltpu.VMEM((1024, BOTH), BF16),
            pltpu.VMEM((1024, BOTH), BF16),
            pltpu.VMEM((BOTH, BOTH), BF16),
            pltpu.VMEM((BOTH, BOTH), BF16),
            pltpu.VMEM((1024, BOTH), BF16),
            pltpu.VMEM((1024, BOTH), BF16),
            pltpu.VMEM((BOTH, 256), BF16),
            pltpu.VMEM((BOTH, 256), BF16),
            pltpu.VMEM((1024, 256), F32),
            dma((15,)), dma((8,)), dma((15,)), dma((8,)), dma((15,)), dma((2,)),
            dma((ITEMS, 7)), dma((ITEMS, 7)), dma((8, 2)), dma((8, 2)), dma((5,)),
        ],
        compiler_params=pltpu.CompilerParams(
            vmem_limit_bytes=62 * 1024 * 1024, collective_id=0, has_side_effects=True
        ),
        cost_estimate=pl.CostEstimate(flops=45_000_000_000, bytes_accessed=18_000_000, transcendentals=0),
        name="panel_factor",
    )(*scal, zr, g)


def per_device(grm, dosages, slab_weight, genetic_var, noise_var):
    scal = (genetic_var, slab_weight, noise_var)
    return factored(scal, dosages.reshape(MS, 1024), grm.reshape(1024, 16, NB)).reshape(grm.shape)


def solution(mesh):
    in_specs = (P(None, "row", None, "col"), P(None, None, "row"), P(), P(), P())
    out_specs = P(None, "row", None, "col")
    return jax.shard_map(
        per_device, mesh=mesh, in_specs=in_specs, out_specs=out_specs, check_vma=False
    )
```
